32 devices in a mesh: dp: 8 (over y, x, core), expert: 4 (over z).
Axes of the slice: x: 2, y: 2, z: 4, core: 2. Of those that a mesh axis runs over, the one named last changes fastest.
Arguments:
- tokens: bfloat16 [96, 2048], P('dp', 'expert'), may hold values from -6 to 6
- cotangent: bfloat16 [96, 2048], P('dp', 'expert'), may hold values from -6 to 6
- route: int32 [96, 2], P('dp'), may hold values from 0 to 3, all different within a row; in each aligned block of 12 rows (0 to 11, 12 to 23, ...) at most 9 rows name the same one
- gates: float32 [96, 2], P('dp'), may hold values from 0.25 to 1
- w_gate: bfloat16 [4, 12288, 2048], P('expert', 'dp'), may hold values from -0.125 to 0.125
- w_up: bfloat16 [4, 12288, 2048], P('expert', 'dp'), may hold values from -0.125 to 0.125
- w_down: bfloat16 [4, 12288, 2048], P('expert', 'dp'), may hold values from -0.0546875 to 0.0546875
Outputs:
- mixed: bfloat16 [96, 2048], P('dp', 'expert')
- grad_tokens: bfloat16 [96, 2048], P('dp', 'expert')
- grad_gate: bfloat16 [4, 12288, 2048], P('expert', 'dp')
- grad_up: bfloat16 [4, 12288, 2048], P('expert', 'dp')
- grad_down: bfloat16 [4, 12288, 2048], P('expert', 'dp')
The draws below stay inside these ranges and needn't reach their ends.
Inputs may be any that keep to these rules, and one draw needn't show every extreme that they name: `route`: the two experts of a token differ. Among the 12 tokens of one index of dp, at most 9 name the same expert, and in some such block one expert is named by exactly 9 tokens. Every expert is named by some token.
All inputs are finite; a program needn't handle non-finite values.
Results may differ from the reference program's by a relative error of at most 0.0065.
Values may be sent and summed in bfloat16 or wider, within the bound.
No kernel may reach another device: no remote copies, remote signals or barrier semaphores. Data moves between devices by JAX's collectives and lax.ppermute only.
A program may use at most 128 MiB of HBM per device.

```python
import math
import jax
import jax.numpy as jnp
import numpy as np
from jax import lax

D = 2048
F = 12288
TOP = 2
TOK_DEV = 12
EXPERTS = 4
CAP = 9
TOKENS = 96
N_DP = 8


def steps_of(stream_key, extent, split, least, top_value):
    level = 1.0
    for position, blocks in split:
        draws = jax.random.uniform(jax.random.fold_in(jax.random.fold_in(stream_key, 6), position), (blocks,), jnp.float32, least / len(split), top_value / len(split))
        level = level * jnp.repeat(jnp.exp(draws), extent[position] // blocks).reshape((-1,) + (1,) * (len(extent) - 1 - position))
    return level


def assign_block(rng, own, number, rows, number_of, top, bound, lean):
    ranking = jax.random.permutation(rng, number_of)
    packed, usual = portions_of(number_of, rows * top, bound, lean, True), portions_of(number_of, rows * top, bound, lean, False)
    places = jnp.arange(number_of)

    def named(sizes, offset_by):
        used = int((sizes > 0).sum())
        fixed = max(1, used // 4)
        passed = fixed + (places - fixed + offset_by * (used - fixed)) % max(1, number_of - fixed)
        return jnp.zeros((number_of,), jnp.int32).at[ranking[jnp.where(places < fixed, places, passed)]].set(jnp.asarray(sizes, jnp.int32))

    sizes = jnp.where(number % 4 == 0, named(packed, number // 4), named(usual, number - number // 4 - 1))
    mixed = jax.random.permutation(jax.random.fold_in(own, 3), number_of)
    giver, taker = mixed[0:number_of // 2 * 2:2], mixed[1:number_of // 2 * 2:2]
    room = jnp.minimum(sizes[giver] - 1, bound - sizes[taker]) // 2
    room = jnp.where((giver == ranking[0]) | (taker == ranking[0]) | (sizes[taker] == 0), 0, jnp.maximum(room, 0))
    passed = jax.random.randint(jax.random.fold_in(own, 4), (number_of // 2,), 0, 1 << 20) % (room + 1)
    sizes = sizes.at[giver].add(-passed).at[taker].add(passed)
    labels = jnp.searchsorted(jnp.cumsum(sizes), jnp.arange(rows * top), side="right").astype(jnp.int32)
    table = labels.reshape(top, rows).T
    table = table[jax.random.permutation(jax.random.fold_in(own, 1), rows)]
    offset_by = jax.random.randint(jax.random.fold_in(own, 2), (rows, 1), 0, top)
    return jnp.take_along_axis(table, (jnp.arange(top)[None, :] + offset_by) % top, axis=1)


def portions_of(number_of, total, limit, lean, full):
    portions = [(1 << 20) // math.isqrt(grade ** lean) + 1 for grade in range(1, number_of + 1)]
    largest = limit if full else min(limit, max(-(-total // number_of), total * portions[0] // sum(portions)))
    least = 1 if total - largest >= number_of - 1 else 0
    given, rest = [largest] + [least] * (number_of - 1), total - largest - least * (number_of - 1)
    while rest > 0:
        movable = [i for i in range(1, number_of) if given[i] < largest] or [i for i in range(1, number_of) if given[i] < limit]
        whole, remaining = sum([portions[i] for i in movable]), rest
        for i in movable:
            addition = min(limit - given[i], max(1, remaining * portions[i] // whole), rest)
            given[i] = given[i] + addition
            rest = rest - addition
    return np.array(given)


def scatter_about(own_key, shape, spread, bound, split=(), kind=jnp.bfloat16):
    entries = spread * jax.random.normal(own_key, shape, jnp.float32)
    if split:
        entries = entries * steps_of(own_key, shape, split, -0.22, 0.18)
    return jnp.clip(entries, -bound, bound).astype(kind)


def setup_inputs(seed: int = 0) -> dict:
    arg_keys = jax.random.split(jax.random.key(seed), 8)
    tokens = scatter_about(arg_keys[0], (TOKENS, D), 1.0, 6.0, ((0, 8), (1, 4)))
    cotangent = scatter_about(arg_keys[1], (TOKENS, D), 1.0, 6.0, ((0, 8), (1, 4)))
    route_keys = jax.random.split(jax.random.fold_in(arg_keys[2], 1), TOKENS // TOK_DEV)
    route_turns = jax.random.permutation(jax.random.fold_in(arg_keys[2], 3), TOKENS // TOK_DEV)
    route = jax.vmap(lambda own, number: assign_block(jax.random.fold_in(arg_keys[2], 2), own, number, TOK_DEV, EXPERTS, TOP, CAP, 2))(route_keys, route_turns).reshape((TOKENS, TOP))
    gates = jnp.clip(0.25 + 0.75 * jax.random.uniform(arg_keys[3], (TOKENS, TOP), jnp.float32) ** steps_of(arg_keys[3], (TOKENS, TOP), ((0, 8),), -0.2, 0.2), 0.25, 1.0)
    w_gate = scatter_about(arg_keys[4], (EXPERTS, F, D), D ** -0.5, 0.125, ((0, 4), (1, 8)))
    w_up = scatter_about(arg_keys[5], (EXPERTS, F, D), D ** -0.5, 0.125, ((0, 4), (1, 8)))
    w_down = scatter_about(arg_keys[6], (EXPERTS, F, D), F ** -0.5, 0.0546875, ((0, 4), (1, 8)))
    return {"tokens": tokens, "cotangent": cotangent, "route": route, "gates": gates, "w_gate": w_gate, "w_up": w_up, "w_down": w_down}


def slots_of(route):
    assign = route.reshape(N_DP, TOP * TOK_DEV)
    order = jnp.arange(TOP * TOK_DEV, dtype=jnp.int32)
    before = order[None, :] < order[:, None]
    same = (assign[:, :, None] == assign[:, None, :]) & before[None]
    slot = jnp.sum(same.astype(jnp.int32), axis=2).astype(jnp.int32)
    return assign, slot


def dispatch(pairs, assign, slot):
    expert_ids = jnp.arange(EXPERTS, dtype=jnp.int32)
    slot_ids = jnp.arange(CAP, dtype=jnp.int32)
    select = ((assign[:, None, None, :] == expert_ids[None, :, None, None])
              & (slot[:, None, None, :] == slot_ids[None, None, :, None])).astype(jnp.float32)
    placed = jnp.einsum('necj,njd->encd', select, pairs.astype(jnp.float32))
    return placed.astype(jnp.bfloat16).reshape(EXPERTS, N_DP * CAP, D)


def contract_rows(left, right):
    return lax.dot_general(left, right, (((0,), (0,)), ((), ())), preferred_element_type=jnp.float32)


def contract_cols(left, right):
    return lax.dot_general(left, right, (((1,), (1,)), ((), ())), preferred_element_type=jnp.float32)


def expert_pass(operands):
    xs, dys, wg, wu, wd = operands
    pre_gate = contract_cols(xs, wg)
    pre_up = contract_cols(xs, wu)
    sig = jax.nn.sigmoid(pre_gate)
    silu = pre_gate * sig
    hidden = (silu * pre_up).astype(jnp.bfloat16)
    expert_out = jnp.dot(hidden, wd, preferred_element_type=jnp.float32).astype(jnp.bfloat16)
    grad_down = contract_rows(hidden, dys).astype(jnp.bfloat16)
    grad_hidden = contract_cols(dys, wd)
    grad_pre_gate = (grad_hidden * pre_up * sig * (1.0 + pre_gate * (1.0 - sig))).astype(jnp.bfloat16)
    grad_pre_up = (grad_hidden * silu).astype(jnp.bfloat16)
    grad_gate = contract_rows(grad_pre_gate, xs).astype(jnp.bfloat16)
    grad_up = contract_rows(grad_pre_up, xs).astype(jnp.bfloat16)
    grad_slots = (jnp.dot(grad_pre_gate, wg, preferred_element_type=jnp.float32)
                  + jnp.dot(grad_pre_up, wu, preferred_element_type=jnp.float32)).astype(jnp.bfloat16)
    return expert_out, grad_slots, grad_gate, grad_up, grad_down


def pick(slot_rows, assign, slot):
    table = slot_rows.reshape(EXPERTS, N_DP, CAP, D)
    blocks = jnp.arange(N_DP, dtype=jnp.int32)[:, None]
    return table[assign, blocks, slot].astype(jnp.float32)


def reference(tokens, cotangent, route, gates, w_gate, w_up, w_down):
    assign, slot = slots_of(route)
    token_pairs = jnp.repeat(tokens.reshape(N_DP, TOK_DEV, D), TOP, axis=1)
    weighted = (gates[:, :, None] * cotangent[:, None, :].astype(jnp.float32)).astype(jnp.bfloat16)
    weighted = weighted.reshape(N_DP, TOP * TOK_DEV, D)
    xs = dispatch(token_pairs, assign, slot)
    dys = dispatch(weighted, assign, slot)
    expert_out, grad_slots, grad_gate, grad_up, grad_down = lax.map(expert_pass, (xs, dys, w_gate, w_up, w_down))
    gate_flat = gates.reshape(N_DP, TOP * TOK_DEV)
    picked = pick(expert_out, assign, slot) * gate_flat[:, :, None]
    mixed = picked.reshape(N_DP, TOK_DEV, TOP, D).sum(axis=2).reshape(TOKENS, D).astype(jnp.bfloat16)
    back = pick(grad_slots, assign, slot)
    grad_tokens = back.reshape(N_DP, TOK_DEV, TOP, D).sum(axis=2).reshape(TOKENS, D).astype(jnp.bfloat16)
    return mixed, grad_tokens, grad_gate, grad_up, grad_down
```

```python
import jax
import jax.numpy as jnp
from jax import lax
from jax.experimental import pallas as pl
from jax.experimental.pallas import tpu as pltpu
from jax.sharding import PartitionSpec as P

BF = jnp.bfloat16
F32 = jnp.float32
VM = pl.BlockSpec(memory_space=pltpu.VMEM)
SM = pl.BlockSpec(memory_space=pltpu.SMEM)
ROWS = 16


def dot_nn(a, b):
    return lax.dot_general(a, b, (((1,), (0,)), ((), ())), preferred_element_type=F32)


def dot_nt(a, b):
    return lax.dot_general(a, b, (((1,), (1,)), ((), ())), preferred_element_type=F32)


def dot_tn(a, b):
    return lax.dot_general(a, b, (((0,), (0,)), ((), ())), preferred_element_type=F32)


def share(route, gates, expert):
    return jnp.sum(jnp.where(route == expert, gates, 0.0), axis=1, keepdims=True)


def params(mib):
    return pltpu.CompilerParams(vmem_limit_bytes=mib << 20)


def pack_kernel(tok_ref, cot_ref, route_ref, gates_ref, out_ref):
    width = tok_ref.shape[1]
    tok = tok_ref[...]
    cot = cot_ref[...].astype(F32)
    route = route_ref[...]
    gates = gates_ref[...]
    for e in range(out_ref.shape[0]):
        out_ref[e, :, :width] = tok
        out_ref[e, :, width:] = (share(route, gates, e) * cot).astype(BF)


def expert_kernel(
    parity_ref, got_ref, wg_ref, wu_ref, wd_ref,
    keep_ref, send_ref, xs_ref, dys_ref, hid_ref, gpg_ref, gpu_ref,
    out_acc, grad_acc,
):
    step = pl.program_id(0)
    n_dp, n_e, tok, pair = got_ref.shape
    width = pair // 2
    d = n_e * width

    @pl.when(step == 0)
    def _():
        xs_ref[...] = jnp.zeros_like(xs_ref)
        dys_ref[...] = jnp.zeros_like(dys_ref)
        for b in range(n_dp):
            for e in range(n_e):
                cols = slice(e * width, (e + 1) * width)
                xs_ref[b * ROWS : b * ROWS + tok, cols] = got_ref[b, e, :, :width]
                dys_ref[b * ROWS : b * ROWS + tok, cols] = got_ref[b, e, :, width:]
        out_acc[...] = jnp.zeros_like(out_acc)
        grad_acc[...] = jnp.zeros_like(grad_acc)

    xs = xs_ref[...]
    dys = dys_ref[...]
    wg = wg_ref[...]
    wu = wu_ref[...]
    wd = wd_ref[...]
    pre_gate = dot_nt(xs, wg)
    pre_up = dot_nt(xs, wu)
    sig = jax.nn.sigmoid(pre_gate)
    silu = pre_gate * sig
    hidden = (silu * pre_up).astype(BF)
    grad_hidden = dot_nt(dys, wd)
    gpg = (grad_hidden * pre_up * sig * (1.0 + pre_gate * (1.0 - sig))).astype(BF)
    gpu = (grad_hidden * silu).astype(BF)
    hid_ref[...] = hidden
    gpg_ref[...] = gpg
    gpu_ref[...] = gpu
    out_acc[...] += dot_nn(hidden, wd)
    grad_acc[...] += dot_nn(gpg, wg) + dot_nn(gpu, wu)

    @pl.when(step == pl.num_programs(0) - 1)
    def _():
        c = parity_ref[0]
        for i in range(n_dp // 2):
            mine = pl.ds(pl.multiple_of((2 * i + c) * ROWS, ROWS), ROWS)
            other = pl.ds(pl.multiple_of((2 * i + 1 - c) * ROWS, ROWS), ROWS)
            keep_ref[i, :, :d] = out_acc[mine, :].astype(BF)
            keep_ref[i, :, d:] = grad_acc[mine, :].astype(BF)
            send_ref[i, :, :d] = out_acc[other, :].astype(BF)
            send_ref[i, :, d:] = grad_acc[other, :].astype(BF)


def weight_grad_kernel(left_ref, right_ref, out_ref):
    out_ref[...] = dot_tn(left_ref[...], right_ref[...]).astype(BF)


def cores_kernel(chip_ref, keep_ref, got_ref, *out_refs):
    chip = chip_ref[0]
    for k, out_ref in enumerate(out_refs):
        i = chip ^ k
        out_ref[...] = (keep_ref[i].astype(F32) + got_ref[i].astype(F32)).astype(BF)


def chips_kernel(*refs):
    out_ref = refs[-1]
    n_e, _, pair = out_ref.shape
    width = pair // 2
    d = n_e * width
    total = refs[0][...].astype(F32)
    for r in refs[1:-1]:
        total = total + r[...].astype(F32)
    total = total.astype(BF)
    for e in range(n_e):
        out_ref[e, :, :width] = total[:, e * width : (e + 1) * width]
        out_ref[e, :, width:] = total[:, d + e * width : d + (e + 1) * width]


def home_kernel(got_ref, route_ref, gates_ref, mixed_ref, grad_ref):
    tok, width = mixed_ref.shape
    route = route_ref[...]
    gates = gates_ref[...]
    mixed = jnp.zeros((tok, width), F32)
    grad = jnp.zeros((tok, width), F32)
    for e in range(got_ref.shape[0]):
        rows = got_ref[e].astype(F32)[:tok]
        mixed = mixed + share(route, gates, e) * rows[:, :width]
        grad = grad + rows[:, width:]
    mixed_ref[...] = mixed.astype(BF)
    grad_ref[...] = grad.astype(BF)


def weight_grad(left, right, tile):
    rows, f = left.shape
    d = right.shape[1]
    return pl.pallas_call(
        weight_grad_kernel,
        grid=(f // tile,),
        in_specs=[
            pl.BlockSpec((rows, tile), lambda i: (0, i)),
            pl.BlockSpec((rows, d), lambda i: (0, 0)),
        ],
        out_specs=pl.BlockSpec((tile, d), lambda i: (i, 0)),
        out_shape=jax.ShapeDtypeStruct((f, d), BF),
        compiler_params=params(24),
        cost_estimate=pl.CostEstimate(
            flops=2 * rows * f * d, bytes_accessed=2 * f * d, transcendentals=0
        ),
        name="weight_grad",
    )(left, right)


def per_device(tokens, cotangent, route, gates, w_gate, w_up, w_down):
    n_dp = lax.axis_size("dp")
    n_e = lax.axis_size("expert")
    tok, width = tokens.shape
    d = width * n_e
    f = w_gate.shape[1]
    tile = 256 if f % 256 == 0 else f
    rows = n_dp * ROWS
    n_chip = n_dp // 2
    me = lax.axis_index("dp").astype(jnp.int32)
    parity = (me % 2).reshape(1)
    chip = (me // 2).reshape(1)
    sds = jax.ShapeDtypeStruct

    packed = pl.pallas_call(
        pack_kernel,
        in_specs=[VM] * 4,
        out_specs=VM,
        out_shape=sds((n_e, tok, 2 * width), BF),
        name="pack",
    )(tokens, cotangent, route, gates)
    packed = lax.all_to_all(packed, "expert", split_axis=0, concat_axis=0, tiled=True)
    got = lax.all_gather(packed, "dp", axis=0, tiled=False)

    weight_spec = pl.BlockSpec((None, tile, d), lambda i: (0, i, 0))
    unit_spec = pl.BlockSpec((rows, tile), lambda i: (0, i))
    keep, send, xs, dys, hidden, gpg, gpu = pl.pallas_call(
        expert_kernel,
        grid=(f // tile,),
        in_specs=[SM, VM] + [weight_spec] * 3,
        out_specs=[VM] * 4 + [unit_spec] * 3,
        out_shape=[sds((n_chip, ROWS, 2 * d), BF)] * 2
        + [sds((rows, d), BF)] * 2
        + [sds((rows, f), BF)] * 3,
        scratch_shapes=[pltpu.VMEM((rows, d), F32)] * 2,
        compiler_params=params(56),
        cost_estimate=pl.CostEstimate(
            flops=12 * rows * f * d, bytes_accessed=6 * f * d, transcendentals=rows * f
        ),
        name="expert",
    )(parity, got, w_gate, w_up, w_down)

    received = lax.ppermute(send, "dp", [(i, i ^ 1) for i in range(n_dp)])
    grad_down = weight_grad(hidden, dys, tile)
    grad_gate = weight_grad(gpg, xs, tile)
    grad_up = weight_grad(gpu, xs, tile)
    parts = pl.pallas_call(
        cores_kernel,
        in_specs=[SM, VM, VM],
        out_specs=[VM] * n_chip,
        out_shape=[sds((ROWS, 2 * d), BF)] * n_chip,
        name="cores",
    )(chip, keep, received)
    arrived = [
        lax.ppermute(parts[k], "dp", [(i, i ^ (2 * k)) for i in range(n_dp)])
        for k in range(1, n_chip)
    ]
    summed = pl.pallas_call(
        chips_kernel,
        in_specs=[VM] * n_chip,
        out_specs=VM,
        out_shape=sds((n_e, ROWS, 2 * width), BF),
        name="chips",
    )(parts[0], *arrived)
    home = lax.all_to_all(summed, "expert", split_axis=0, concat_axis=0, tiled=True)
    mixed, grad_tokens = pl.pallas_call(
        home_kernel,
        in_specs=[VM] * 3,
        out_specs=[VM] * 2,
        out_shape=[sds((tok, width), BF)] * 2,
        name="home",
    )(home, route, gates)
    return mixed, grad_tokens, grad_gate[None], grad_up[None], grad_down[None]


def solution(mesh):
    return jax.shard_map(
        per_device,
        mesh=mesh,
        in_specs=(
            P("dp", "expert"),
            P("dp", "expert"),
            P("dp", None),
            P("dp", None),
            P("expert", "dp", None),
            P("expert", "dp", None),
            P("expert", "dp", None),
        ),
        out_specs=(
            P("dp", "expert"),
            P("dp", "expert"),
            P("expert", "dp", None),
            P("expert", "dp", None),
            P("expert", "dp", None),
        ),
        check_vma=False,
    )
```

```python
import functools

import jax
import jax.numpy as jnp
from jax import lax
from jax.experimental import pallas as pl
from jax.experimental.pallas import tpu as pltpu
from jax.sharding import PartitionSpec as P

BF = jnp.bfloat16
F32 = jnp.float32
VM = pl.BlockSpec(memory_space=pltpu.VMEM)
HBM = pl.BlockSpec(memory_space=pltpu.HBM)
ANY = pl.BlockSpec(memory_space=pl.ANY)
ROWS = 16


def dot_nn(a, b):
    return lax.dot_general(a, b, (((1,), (0,)), ((), ())), preferred_element_type=F32)


def dot_nt(a, b):
    return lax.dot_general(a, b, (((1,), (1,)), ((), ())), preferred_element_type=F32)


def dot_tn(a, b):
    return lax.dot_general(a, b, (((0,), (0,)), ((), ())), preferred_element_type=F32)


def share(route, gates, expert):
    tok = route.shape[1]
    row = jnp.sum(jnp.where(route == expert, gates, 0.0), axis=0, keepdims=True)
    square = jnp.broadcast_to(row, (tok, tok))
    diagonal = lax.broadcasted_iota(jnp.int32, (tok, tok), 0) == lax.broadcasted_iota(
        jnp.int32, (tok, tok), 1
    )
    return jnp.sum(jnp.where(diagonal, square, 0.0), axis=1, keepdims=True)


def params(mib):
    return pltpu.CompilerParams(vmem_limit_bytes=mib << 20)


def pack_kernel(
    tok_hbm, cot_hbm, route_hbm, gates_hbm, *refs
):
    outs, (tok_ref, cot_ref, route_ref, gates_ref, sems) = refs[:-5], refs[-5:]
    pairs = (
        (tok_hbm, tok_ref), (cot_hbm, cot_ref), (route_hbm, route_ref), (gates_hbm, gates_ref)
    )
    copies = [pltpu.make_async_copy(a, b, sems.at[i]) for i, (a, b) in enumerate(pairs)]
    for copy in copies:
        copy.start()
    for copy in copies:
        copy.wait()
    tok, width = tok_ref.shape
    token_rows = tok_ref[...]
    cot = cot_ref[...].astype(F32)
    route = route_ref[...]
    gates = gates_ref[...]
    me = lax.axis_index("expert")
    for k, out_ref in enumerate(outs):
        out_ref[...] = jnp.zeros_like(out_ref)
        out_ref[:tok, :width] = token_rows
        out_ref[:tok, width:] = (share(route, gates, me ^ k) * cot).astype(BF)


def load_kernel(after_ref, *refs):
    n = (len(refs) - 1) // 2
    sems = refs[-1]
    copies = [pltpu.make_async_copy(refs[i], refs[n + i], sems.at[i]) for i in range(n)]
    for copy in copies:
        copy.start()
    for copy in copies:
        copy.wait()


def join_kernel(*refs):
    ins, out_ref = refs[:-1], refs[-1]
    width = ins[0].shape[1] // 2
    d = len(ins) * width
    me = lax.axis_index("expert")
    for e in range(len(ins)):
        for k, ref in enumerate(ins):

            @pl.when(me ^ k == e)
            def _(e=e, ref=ref):
                out_ref[:, e * width : (e + 1) * width] = ref[:, :width]
                out_ref[:, d + e * width : d + (e + 1) * width] = ref[:, width:]


def stack_kernel(*refs):
    out_ref = refs[-1]
    for k, ref in enumerate(refs[:-1]):
        out_ref[k * ROWS : (k + 1) * ROWS] = ref[...]


def expert_kernel(
    near_ref, far_ref, wg_ref, wu_ref, wd_ref,
    keep_ref, send_ref, xs_ref, dys_ref, hidt_ref, gpgt_ref, gput_ref,
    hid_ref, gpg_ref, gpu_ref,
    *, tile, cols,
):
    half = near_ref.shape[0]
    f, d = wg_ref.shape
    xs_ref[:half] = near_ref[:, :d]
    xs_ref[half:] = far_ref[:, :d]
    dys_ref[:half] = near_ref[:, d:]
    dys_ref[half:] = far_ref[:, d:]
    xs = xs_ref[...]
    dys = dys_ref[...]
    for i in range(f // tile):
        units = slice(i * tile, (i + 1) * tile)
        pre_gate = dot_nt(xs, wg_ref[units, :])
        pre_up = dot_nt(xs, wu_ref[units, :])
        grad_hidden = dot_nt(dys, wd_ref[units, :])
        sig = jax.nn.sigmoid(pre_gate)
        silu = pre_gate * sig
        hidden = (silu * pre_up).astype(BF)
        gpg = (grad_hidden * pre_up * sig * (1.0 + pre_gate * (1.0 - sig))).astype(BF)
        gpu = (grad_hidden * silu).astype(BF)
        hid_ref[:, units] = hidden
        gpg_ref[:, units] = gpg
        gpu_ref[:, units] = gpu
        hidt_ref[units, :] = hidden.T
        gpgt_ref[units, :] = gpg.T
        gput_ref[units, :] = gpu.T
    hidden = hid_ref[...]
    gpg = gpg_ref[...]
    gpu = gpu_ref[...]
    for j in range(d // cols):
        part = slice(j * cols, (j + 1) * cols)
        out = dot_nn(hidden, wd_ref[:, part]).astype(BF)
        grad = (dot_nn(gpg, wg_ref[:, part]) + dot_nn(gpu, wu_ref[:, part])).astype(BF)
        for at, value in ((j * cols, out), (d + j * cols, grad)):
            keep_ref[:, at : at + cols] = value[:half]
            send_ref[:, at : at + cols] = value[half:]


def grads_kernel(jobs, n, n_old, *refs):
    lefts, rights = refs[:n], refs[n : 2 * n]
    outs, (buf, sems) = refs[2 * n + n_old : 3 * n + n_old], refs[3 * n + n_old :]
    slots = buf.shape[0]
    copies = []
    for i, (a, start, size) in enumerate(jobs):
        slot = i % slots
        if i >= slots:
            copies[i - slots].wait()
        rows = pl.ds(start, size)
        buf[slot, :size] = dot_nn(lefts[a][rows, :], rights[a][...]).astype(BF)
        copy = pltpu.make_async_copy(buf.at[slot, pl.ds(0, size)], outs[a].at[rows, :], sems.at[slot])
        copy.start()
        copies.append(copy)
    for copy in copies[-slots:]:
        copy.wait()


def cores_kernel(keep_ref, got_ref, *out_refs):
    for k, out_ref in enumerate(out_refs):
        rows = slice(k * ROWS, (k + 1) * ROWS)
        out_ref[...] = (keep_ref[rows].astype(F32) + got_ref[rows].astype(F32)).astype(BF)


def chips_kernel(n, *refs):
    ins, outs = refs[:n], refs[n:]
    width = outs[0].shape[1] // 2
    d = len(outs) * width
    total = ins[0][...].astype(F32)
    for ref in ins[1:]:
        total = total + ref[...].astype(F32)
    total = total.astype(BF)
    me = lax.axis_index("expert")
    for e in range(len(outs)):
        for k, out_ref in enumerate(outs):

            @pl.when(me ^ k == e)
            def _(e=e, out_ref=out_ref):
                out_ref[:, :width] = total[:, e * width : (e + 1) * width]
                out_ref[:, width:] = total[:, d + e * width : d + (e + 1) * width]


def home_kernel(*refs):
    ins, (route_ref, gates_ref, mixed_ref, grad_ref) = refs[:-4], refs[-4:]
    tok, width = mixed_ref.shape
    route = route_ref[...]
    gates = gates_ref[...]
    mixed = jnp.zeros((tok, width), F32)
    grad = jnp.zeros((tok, width), F32)
    me = lax.axis_index("expert")
    for k, ref in enumerate(ins):
        got = ref[...].astype(F32)[:tok]
        mixed = mixed + share(route, gates, me ^ k) * got[:, :width]
        grad = grad + got[:, width:]
    mixed_ref[...] = mixed.astype(BF)
    grad_ref[...] = grad.astype(BF)


def grads(jobs, lefts, rights, old):
    n = len(lefts)
    f, rows = lefts[0].shape
    d = rights[0].shape[1]
    kept = [a for a in range(n) if old[a] is not None]
    size = max(job[2] for job in jobs)
    done = sum(job[2] for job in jobs)
    return pl.pallas_call(
        functools.partial(grads_kernel, jobs, n, len(kept)),
        in_specs=[VM] * (2 * n) + [HBM] * len(kept),
        out_specs=[HBM] * n,
        out_shape=[jax.ShapeDtypeStruct((f, d), BF)] * n,
        scratch_shapes=[pltpu.VMEM((3, size, d), BF), pltpu.SemaphoreType.DMA((3,))],
        input_output_aliases={2 * n + i: a for i, a in enumerate(kept)},
        compiler_params=params(((6 * size * d + n * 2 * rows * (f + d)) >> 20) + 4),
        cost_estimate=pl.CostEstimate(
            flops=2 * rows * done * d, bytes_accessed=3 * done * d, transcendentals=0
        ),
        name="grads",
    )(*lefts, *rights, *[old[a] for a in kept])


def load(mib, after, *arrays):
    size = sum(a.size for a in arrays) * 2
    return pl.pallas_call(
        load_kernel,
        in_specs=[ANY] + [HBM] * len(arrays),
        out_specs=[VM] * len(arrays),
        out_shape=[jax.ShapeDtypeStruct(a.shape, a.dtype) for a in arrays],
        scratch_shapes=[pltpu.SemaphoreType.DMA((len(arrays),))],
        compiler_params=params(mib),
        cost_estimate=pl.CostEstimate(flops=0, bytes_accessed=size, transcendentals=0),
        name="load",
    )(after, *arrays)


def stack(kernel, arrays, shape, name):
    size = 2 * sum(a.size for a in arrays)
    return pl.pallas_call(
        kernel,
        in_specs=[VM] * len(arrays),
        out_specs=VM,
        out_shape=jax.ShapeDtypeStruct(shape, BF),
        compiler_params=params((size >> 19) + 2),
        name=name,
    )(*arrays)


def per_device(tokens, cotangent, route, gates, w_gate, w_up, w_down):
    n_dp = lax.axis_size("dp")
    n_e = lax.axis_size("expert")
    tok, width = tokens.shape
    d = width * n_e
    f = w_gate.shape[1]
    tile = 256 if f % 256 == 0 else f
    rows = n_dp * ROWS
    n_chip = n_dp // 2
    sds = jax.ShapeDtypeStruct

    def swap(x, axis, size, k):
        return lax.ppermute(x, axis, [(i, i ^ k) for i in range(size)])

    small = n_chip + 4
    packed = pl.pallas_call(
        pack_kernel,
        in_specs=[HBM] * 4,
        out_specs=[VM] * n_e,
        out_shape=[sds((ROWS, 2 * width), BF)] * n_e,
        scratch_shapes=[
            pltpu.VMEM(tokens.shape, BF),
            pltpu.VMEM(tokens.shape, BF),
            pltpu.VMEM((2, tok), jnp.int32),
            pltpu.VMEM((2, tok), F32),
            pltpu.SemaphoreType.DMA((4,)),
        ],
        name="pack",
    )(tokens, cotangent, route.T, gates.T)
    mine = [packed[0]] + [swap(packed[k], "expert", n_e, k) for k in range(1, n_e)]
    weight_mib = f * d >> 19
    (wg,) = load(weight_mib + 3, packed[0], w_gate[0])
    mine, wg = lax.optimization_barrier((mine, wg))
    block = stack(join_kernel, mine, (ROWS, 2 * d), "join")
    blocks = [block] + [swap(block, "dp", n_dp, 2 * k) for k in range(1, n_chip)]
    wu, wd = load(2 * weight_mib + 3, block, w_up[0], w_down[0])
    blocks, wu, wd = lax.optimization_barrier((blocks, wu, wd))
    near = stack(stack_kernel, blocks, (n_chip * ROWS, 2 * d), "stack")
    far = swap(near, "dp", n_dp, 1)

    held = 2 * f * d + rows * (16 * d + 12 * f)
    keep, send, xs, dys, hidden, gpg, gpu = pl.pallas_call(
        functools.partial(expert_kernel, tile=tile, cols=256),
        in_specs=[VM] * 5,
        out_specs=[VM] * 7,
        out_shape=[sds((n_chip * ROWS, 2 * d), BF)] * 2
        + [sds((rows, d), BF)] * 2
        + [sds((f, rows), BF)] * 3,
        scratch_shapes=[pltpu.VMEM((rows, f), BF)] * 3,
        compiler_params=params((held >> 20) + 4),
        cost_estimate=pl.CostEstimate(
            flops=12 * rows * f * d, bytes_accessed=6 * f * d, transcendentals=rows * f
        ),
        name="expert",
    )(near, far, wg, wu, wd)

    received = swap(send, "dp", n_dp, 1)
    third = f // 3
    whole = [(1, i * third, third) for i in range(3)]
    (down,) = grads([(0, 0, third)], [hidden], [dys], [None])
    received, down = lax.optimization_barrier((received, down))
    parts = pl.pallas_call(
        cores_kernel,
        in_specs=[VM, VM],
        out_specs=[VM] * n_chip,
        out_shape=[sds((ROWS, 2 * d), BF)] * n_chip,
        compiler_params=params(small),
        name="cores",
    )(keep, received)
    arrived = [swap(parts[k], "dp", n_dp, 2 * k) for k in range(1, n_chip)]
    down, grad_gate = grads([(0, third, third)] + whole, [hidden, gpg], [dys, xs], [down, None])
    arrived, down, grad_gate = lax.optimization_barrier((arrived, down, grad_gate))
    summed = pl.pallas_call(
        functools.partial(chips_kernel, n_chip),
        in_specs=[VM] * n_chip,
        out_specs=[VM] * n_e,
        out_shape=[sds((ROWS, 2 * width), BF)] * n_e,
        compiler_params=params(small),
        name="chips",
    )(parts[0], *arrived)
    home = [summed[0]] + [swap(summed[k], "expert", n_e, k) for k in range(1, n_e)]
    grad_down, grad_up = grads(
        [(0, 2 * third, third)] + whole, [hidden, gpu], [dys, xs], [down, None]
    )
    home, grad_down, grad_up = lax.optimization_barrier((home, grad_down, grad_up))
    mixed, grad_tokens = pl.pallas_call(
        home_kernel,
        in_specs=[VM] * (n_e + 2),
        out_specs=[VM] * 2,
        out_shape=[sds((tok, width), BF)] * 2,
        compiler_params=params(4),
        name="home",
    )(*home, route.T, gates.T)
    return mixed, grad_tokens, grad_gate[None], grad_up[None], grad_down[None]


def solution(mesh):
    return jax.shard_map(
        per_device,
        mesh=mesh,
        in_specs=(
            P("dp", "expert"),
            P("dp", "expert"),
            P("dp", None),
            P("dp", None),
            P("expert", "dp", None),
            P("expert", "dp", None),
            P("expert", "dp", None),
        ),
        out_specs=(
            P("dp", "expert"),
            P("dp", "expert"),
            P("expert", "dp", None),
            P("expert", "dp", None),
            P("expert", "dp", None),
        ),
        check_vma=False,
    )
```

```python
import functools

import jax
import jax.numpy as jnp
from jax import lax
from jax.experimental import pallas as pl
from jax.experimental.pallas import tpu as pltpu
from jax.sharding import PartitionSpec as P

BF = jnp.bfloat16
F32 = jnp.float32
VM = pl.BlockSpec(memory_space=pltpu.VMEM)
HBM = pl.BlockSpec(memory_space=pltpu.HBM)
ROWS = 16


def dot_nn(a, b):
    return lax.dot_general(a, b, (((1,), (0,)), ((), ())), preferred_element_type=F32)


def dot_nt(a, b):
    return lax.dot_general(a, b, (((1,), (1,)), ((), ())), preferred_element_type=F32)


def dot_tn(a, b):
    return lax.dot_general(a, b, (((0,), (0,)), ((), ())), preferred_element_type=F32)


def share(route, gates, expert):
    tok = route.shape[1]
    row = jnp.sum(jnp.where(route == expert, gates, 0.0), axis=0, keepdims=True)
    square = jnp.broadcast_to(row, (tok, tok))
    diagonal = lax.broadcasted_iota(jnp.int32, (tok, tok), 0) == lax.broadcasted_iota(
        jnp.int32, (tok, tok), 1
    )
    return jnp.sum(jnp.where(diagonal, square, 0.0), axis=1, keepdims=True)


def params(mib):
    return pltpu.CompilerParams(vmem_limit_bytes=mib << 20)


def share_kernel(route_ref, gates_ref, out_ref):
    tok = route_ref.shape[1]
    out_ref[...] = jnp.zeros_like(out_ref)
    column = share(route_ref[...], gates_ref[...], lax.axis_index("expert"))
    out_ref[:tok] = jnp.broadcast_to(column, (tok, out_ref.shape[1]))


def pair_kernel(a_ref, b_ref, out_ref):
    n = a_ref.shape[0]
    out_ref[:n] = a_ref[...]
    out_ref[n:] = b_ref[...]


def join_kernel(patterns, share_ref, a_ref, b_ref, out_ref):
    half, tok, width = a_ref.shape
    width //= 2
    d = len(patterns) * width
    me = lax.axis_index("expert")
    weight = share_ref[:tok, :1]
    out_ref[...] = jnp.zeros_like(out_ref)
    for i, k in enumerate(patterns):
        block = a_ref[i] if i < half else b_ref[i - half]
        dys = (weight * block[:, width:].astype(F32)).astype(BF)
        for e in range(len(patterns)):

            @pl.when(me ^ k == e)
            def _(e=e, block=block, dys=dys):
                out_ref[:tok, e * width : (e + 1) * width] = block[:, :width]
                out_ref[:tok, d + e * width : d + (e + 1) * width] = dys


def stack_kernel(*refs):
    out_ref = refs[-1]
    for k, ref in enumerate(refs[:-1]):
        out_ref[k * ROWS : (k + 1) * ROWS] = ref[...]


def expert_kernel(
    near_ref, far_ref, wg_ref, wu_ref, wd_ref,
    keep_ref, send_ref, xs_ref, dys_ref, hidt_ref, gpgt_ref, gput_ref,
    hid_ref, gpg_ref, gpu_ref,
    *, tile, cols,
):
    half = near_ref.shape[0]
    f, d = wg_ref.shape
    xs_ref[:half] = near_ref[:, :d]
    xs_ref[half:] = far_ref[:, :d]
    dys_ref[:half] = near_ref[:, d:]
    dys_ref[half:] = far_ref[:, d:]
    xs = xs_ref[...]
    dys = dys_ref[...]
    for i in range(f // tile):
        units = slice(i * tile, (i + 1) * tile)
        pre_gate = dot_nt(xs, wg_ref[units, :])
        pre_up = dot_nt(xs, wu_ref[units, :])
        grad_hidden = dot_nt(dys, wd_ref[units, :])
        sig = jax.nn.sigmoid(pre_gate)
        silu = pre_gate * sig
        hidden = (silu * pre_up).astype(BF)
        gpg = (grad_hidden * pre_up * sig * (1.0 + pre_gate * (1.0 - sig))).astype(BF)
        gpu = (grad_hidden * silu).astype(BF)
        hid_ref[:, units] = hidden
        gpg_ref[:, units] = gpg
        gpu_ref[:, units] = gpu
        hidt_ref[units, :] = hidden.T
        gpgt_ref[units, :] = gpg.T
        gput_ref[units, :] = gpu.T
    hidden = hid_ref[...]
    gpg = gpg_ref[...]
    gpu = gpu_ref[...]
    for j in range(d // cols):
        part = slice(j * cols, (j + 1) * cols)
        out = dot_nn(hidden, wd_ref[:, part]).astype(BF)
        grad = (dot_nn(gpg, wg_ref[:, part]) + dot_nn(gpu, wu_ref[:, part])).astype(BF)
        for at, value in ((j * cols, out), (d + j * cols, grad)):
            keep_ref[:, at : at + cols] = value[:half]
            send_ref[:, at : at + cols] = value[half:]


def grads_kernel(jobs, n, n_old, *refs):
    lefts, rights = refs[:n], refs[n : 2 * n]
    outs, (buf, sems) = refs[2 * n + n_old : 3 * n + n_old], refs[3 * n + n_old :]
    slots = buf.shape[0]
    copies = []
    for i, (a, start, size) in enumerate(jobs):
        slot = i % slots
        if i >= slots:
            copies[i - slots].wait()
        rows = pl.ds(start, size)
        buf[slot, :size] = dot_nn(lefts[a][rows, :], rights[a][...]).astype(BF)
        copy = pltpu.make_async_copy(buf.at[slot, pl.ds(0, size)], outs[a].at[rows, :], sems.at[slot])
        copy.start()
        copies.append(copy)
    for copy in copies[-slots:]:
        copy.wait()


def cores_kernel(keep_ref, got_ref, *out_refs):
    for k, out_ref in enumerate(out_refs):
        rows = slice(k * ROWS, (k + 1) * ROWS)
        out_ref[...] = (keep_ref[rows].astype(F32) + got_ref[rows].astype(F32)).astype(BF)


def chips_kernel(n, share_ref, *refs):
    ins, outs = refs[:n], refs[n:]
    width = outs[0].shape[1] // 2
    d = len(outs) * width
    total = ins[0][...].astype(F32)
    for ref in ins[1:]:
        total = total + ref[...].astype(F32)
    out = (share_ref[:, :1] * total[:, :d]).astype(BF)
    grad = total[:, d:].astype(BF)
    me = lax.axis_index("expert")
    for e in range(len(outs)):
        part = slice(e * width, (e + 1) * width)
        for k, out_ref in enumerate(outs):

            @pl.when(me ^ k == e)
            def _(part=part, out_ref=out_ref):
                out_ref[:, :width] = out[:, part]
                out_ref[:, width:] = grad[:, part]


def home_kernel(*refs):
    ins, (mixed_ref, grad_ref) = refs[:-2], refs[-2:]
    tok, width = mixed_ref.shape
    total = ins[0][...].astype(F32)
    for ref in ins[1:]:
        total = total + ref[...].astype(F32)
    mixed_ref[...] = total[:tok, :width].astype(BF)
    grad_ref[...] = total[:tok, width:].astype(BF)


def grads(jobs, lefts, rights, old):
    n = len(lefts)
    f, rows = lefts[0].shape
    d = rights[0].shape[1]
    kept = [a for a in range(n) if old[a] is not None]
    size = max(job[2] for job in jobs)
    done = sum(job[2] for job in jobs)
    return pl.pallas_call(
        functools.partial(grads_kernel, jobs, n, len(kept)),
        in_specs=[VM] * (2 * n) + [HBM] * len(kept),
        out_specs=[HBM] * n,
        out_shape=[jax.ShapeDtypeStruct((f, d), BF)] * n,
        scratch_shapes=[pltpu.VMEM((3, size, d), BF), pltpu.SemaphoreType.DMA((3,))],
        input_output_aliases={2 * n + i: a for i, a in enumerate(kept)},
        compiler_params=params(((6 * size * d + n * 2 * rows * (f + d)) >> 20) + 4),
        cost_estimate=pl.CostEstimate(
            flops=2 * rows * done * d, bytes_accessed=3 * done * d, transcendentals=0
        ),
        name="grads",
    )(*lefts, *rights, *[old[a] for a in kept])


def stack(kernel, arrays, shape, name, dtype=BF):
    size = sum(a.size * a.dtype.itemsize for a in arrays)
    return pl.pallas_call(
        kernel,
        in_specs=[VM] * len(arrays),
        out_specs=VM,
        out_shape=jax.ShapeDtypeStruct(shape, dtype),
        compiler_params=params((size >> 19) + 2),
        name=name,
    )(*arrays)


def per_device(tokens, cotangent, route, gates, w_gate, w_up, w_down):
    n_dp = lax.axis_size("dp")
    n_e = lax.axis_size("expert")
    tok, width = tokens.shape
    d = width * n_e
    f = w_gate.shape[1]
    tile = 256 if f % 256 == 0 else f
    rows = n_dp * ROWS
    n_chip = n_dp // 2
    sds = jax.ShapeDtypeStruct

    def swap(x, axis, size, k):
        return lax.ppermute(x, axis, [(i, i ^ k) for i in range(size)])

    small = n_chip + 4
    mine = jnp.concatenate([tokens, cotangent], axis=1)[None]
    patterns, hop, first = [0], n_e // 2, True
    while hop:
        patterns = patterns + [p ^ hop for p in patterns]
        got = swap(mine, "expert", n_e, hop)
        if first:
            weight = pl.pallas_call(
                share_kernel,
                in_specs=[VM, VM],
                out_specs=VM,
                out_shape=sds((ROWS, 128), F32),
                compiler_params=params(2),
                cost_estimate=pl.CostEstimate(
                    flops=40 * rows * f * d, bytes_accessed=24 * f * d, transcendentals=0
                ),
                name="share",
            )(route.T, gates.T)
            first = False
            got, weight = lax.optimization_barrier((got, weight))
        if hop == 1:
            block = stack(
                functools.partial(join_kernel, tuple(patterns)),
                [weight, mine, got],
                (ROWS, 2 * d),
                "join",
            )
        else:
            mine = stack(pair_kernel, [mine, got], (len(patterns), tok, 2 * width), "pair")
        hop //= 2
    blocks = [block] + [swap(block, "dp", n_dp, 2 * k) for k in range(1, n_chip)]
    near = stack(stack_kernel, blocks, (n_chip * ROWS, 2 * d), "stack")
    far = swap(near, "dp", n_dp, 1)

    held = 2 * f * d + rows * (16 * d + 12 * f)
    keep, send, xs, dys, hidden, gpg, gpu = pl.pallas_call(
        functools.partial(expert_kernel, tile=tile, cols=256),
        in_specs=[VM] * 5,
        out_specs=[VM] * 7,
        out_shape=[sds((n_chip * ROWS, 2 * d), BF)] * 2
        + [sds((rows, d), BF)] * 2
        + [sds((f, rows), BF)] * 3,
        scratch_shapes=[pltpu.VMEM((rows, f), BF)] * 3,
        compiler_params=params((held >> 20) + 4),
        cost_estimate=pl.CostEstimate(
            flops=12 * rows * f * d, bytes_accessed=6 * f * d, transcendentals=rows * f
        ),
        name="expert",
    )(near, far, w_gate[0], w_up[0], w_down[0])

    received = swap(send, "dp", n_dp, 1)
    third, sixth = f // 3, f // 6
    whole = [(1, i * third, third) for i in range(3)]
    (down,) = grads([(0, 0, sixth)], [hidden], [dys], [None])
    received, down = lax.optimization_barrier((received, down))
    parts = pl.pallas_call(
        cores_kernel,
        in_specs=[VM, VM],
        out_specs=[VM] * n_chip,
        out_shape=[sds((ROWS, 2 * d), BF)] * n_chip,
        compiler_params=params(small),
        name="cores",
    )(keep, received)
    arrived = [swap(parts[k], "dp", n_dp, 2 * k) for k in range(n_chip - 1, 0, -1)]
    down, grad_gate = grads([(0, sixth, third), (0, 3 * sixth, third)] + whole, [hidden, gpg], [dys, xs], [down, None])
    arrived, down, grad_gate = lax.optimization_barrier((arrived, down, grad_gate))
    summed = pl.pallas_call(
        functools.partial(chips_kernel, n_chip),
        in_specs=[VM] * (n_chip + 1),
        out_specs=[VM] * n_e,
        out_shape=[sds((ROWS, 2 * width), BF)] * n_e,
        compiler_params=params(small),
        name="chips",
    )(weight, parts[0], *arrived)
    home = [summed[0]] + [swap(summed[k], "expert", n_e, k) for k in range(n_e - 1, 0, -1)]
    grad_down, grad_up = grads(
        [(0, 5 * sixth, sixth)] + whole, [hidden, gpu], [dys, xs], [down, None]
    )
    home, grad_down, grad_up = lax.optimization_barrier((home, grad_down, grad_up))
    mixed, grad_tokens = pl.pallas_call(
        home_kernel,
        in_specs=[VM] * n_e,
        out_specs=[VM] * 2,
        out_shape=[sds((tok, width), BF)] * 2,
        compiler_params=params(4),
        name="home",
    )(*home)
    return mixed, grad_tokens, grad_gate[None], grad_up[None], grad_down[None]


def solution(mesh):
    return jax.shard_map(
        per_device,
        mesh=mesh,
        in_specs=(
            P("dp", "expert"),
            P("dp", "expert"),
            P("dp", None),
            P("dp", None),
            P("expert", "dp", None),
            P("expert", "dp", None),
            P("expert", "dp", None),
        ),
        out_specs=(
            P("dp", "expert"),
            P("dp", "expert"),
            P("expert", "dp", None),
            P("expert", "dp", None),
            P("expert", "dp", None),
        ),
        check_vma=False,
    )
```

```python
import functools

import jax
import jax.numpy as jnp
from jax import lax
from jax.experimental import pallas as pl
from jax.experimental.pallas import tpu as pltpu
from jax.sharding import PartitionSpec as P

BF = jnp.bfloat16
F32 = jnp.float32
VM = pl.BlockSpec(memory_space=pltpu.VMEM)
HBM = pl.BlockSpec(memory_space=pltpu.HBM)
ROWS = 16
EIGHT = 8


def dot_nn(a, b):
    return lax.dot_general(a, b, (((1,), (0,)), ((), ())), preferred_element_type=F32)


def dot_nt(a, b):
    return lax.dot_general(a, b, (((1,), (1,)), ((), ())), preferred_element_type=F32)


def dot_tn(a, b):
    return lax.dot_general(a, b, (((0,), (0,)), ((), ())), preferred_element_type=F32)


def params(mib):
    return pltpu.CompilerParams(vmem_limit_bytes=mib << 20)


def share_kernel(route_ref, gates_ref, out_ref):
    tok = route_ref.shape[1]
    lanes = out_ref.shape[1]
    hit = route_ref[...] == lax.axis_index("expert")
    routed = jnp.sum(jnp.where(hit, 1.0, 0.0), axis=0, keepdims=True)
    gate = jnp.sum(jnp.where(hit, gates_ref[...], 0.0), axis=0, keepdims=True)
    row = lax.broadcasted_iota(jnp.int32, (tok, tok), 0)
    col = lax.broadcasted_iota(jnp.int32, (tok, tok), 1)
    square = jnp.broadcast_to(routed, (tok, tok))
    routed_col = jnp.sum(jnp.where(row == col, square, 0.0), axis=1, keepdims=True)
    slot_col = jnp.sum(jnp.where(col < row, square, 0.0), axis=1, keepdims=True)
    slot = jnp.sum(jnp.where(row < col, routed_col, 0.0), axis=0, keepdims=True)
    at = lax.broadcasted_iota(jnp.int32, (ROWS, tok), 0).astype(F32)
    pick = jnp.where(at == slot, routed, 0.0)
    weight = jnp.sum(pick * gate, axis=1, keepdims=True)
    out_ref[...] = jnp.zeros_like(out_ref)
    out_ref[:ROWS] = jnp.broadcast_to(weight, (ROWS, lanes))
    out_ref[ROWS : 2 * ROWS, :tok] = pick
    at = lax.broadcasted_iota(jnp.int32, (tok, lanes), 1).astype(F32)
    out_ref[2 * ROWS : 2 * ROWS + tok] = jnp.where(at == slot_col, routed_col, 0.0)


def odd(k):
    return (k ^ (k >> 1) ^ (k >> 2)) & 1


def extra_place(column, extra, d):
    piece = 2 * d // EIGHT
    if isinstance(column, int):
        return column // piece, extra * piece + column % piece
    return lax.div(column, piece), extra * piece + lax.rem(column, piece)


def lanes_at(column, width):
    if not isinstance(column, int):
        column = pl.multiple_of(column, 128)
    return pl.ds(column, width)


def pair_kernel(a_ref, b_ref, out_ref):
    n = a_ref.shape[0]
    out_ref[:n] = a_ref[...]
    out_ref[n:] = b_ref[...]


def join_kernel(patterns, slots, mine_ref, other_ref, a_ref, b_ref, out_ref, tail_ref):
    half, tok, width = a_ref.shape
    width //= 2
    d = len(patterns) * width
    me = lax.axis_index("expert")
    for i, k in enumerate(patterns):
        info = other_ref if odd(k) else mine_ref
        block = a_ref[i] if i < half else b_ref[i - half]
        picked = dot_nn(info[ROWS : 2 * ROWS, :tok].astype(BF), block)
        dys = info[:ROWS, :1] * picked[:, width:]
        for at, rows in ((0, picked[:, :width]), (d, dys)):
            column = at + (me ^ k) * width
            out_ref[:, lanes_at(column, width)] = rows[:EIGHT].astype(BF)
            for x in range(slots - EIGHT):
                r, c = extra_place(column, x, d)
                tail_ref[pl.ds(r, 1), lanes_at(c, width)] = rows[EIGHT + x : EIGHT + x + 1]
    if slots > EIGHT:
        out_ref[:, 2 * d :] = tail_ref[...].astype(BF)


def stack_kernel(*refs):
    out_ref = refs[-1]
    for k, ref in enumerate(refs[:-1]):
        out_ref[k] = ref[...]


def expert_kernel(
    near_ref, far_ref, wg_ref, wu_ref, wd_ref,
    keep_ref, send_ref, xs_ref, dys_ref, hidt_ref, gpgt_ref, gput_ref,
    hid_ref, gpg_ref, gpu_ref, tail_ref,
    *, tile, cols, slots,
):
    n = near_ref.shape[0]
    f, d = wg_ref.shape
    width = d // lax.axis_size("expert")
    piece = 2 * d // EIGHT
    me = lax.axis_index("expert")
    first = lax.broadcasted_iota(jnp.int32, (EIGHT, width), 0)
    for j in range(d // width):
        for crossed in range(2):

            @pl.when(odd(me ^ j) == crossed)
            def _(j=j, crossed=crossed):
                for b in range(n):
                    near, far = near_ref.at[b], far_ref.at[b]
                    if crossed ^ (b > 0):
                        near, far = far, near
                    for at, ref in ((b * ROWS, near), ((n + b) * ROWS, far)):
                        for base, to in ((0, xs_ref), (d, dys_ref)):
                            part = slice(j * width, (j + 1) * width)
                            column = base + j * width
                            to[at : at + EIGHT, part] = ref[:, column : column + width]
                            rest = jnp.zeros((EIGHT, width), F32)
                            for x in range(slots - EIGHT):
                                r, c = extra_place(column, x, d)
                                tail = ref[:, 2 * d + c : 2 * d + c + width].astype(F32)
                                rest = jnp.where(first == x, tail[r : r + 1], rest)
                            to[at + EIGHT : at + ROWS, part] = rest.astype(BF)

    xs = xs_ref[...]
    dys = dys_ref[...]
    for i in range(f // tile):
        units = slice(i * tile, (i + 1) * tile)
        pre_gate = dot_nt(xs, wg_ref[units, :])
        pre_up = dot_nt(xs, wu_ref[units, :])
        grad_hidden = dot_nt(dys, wd_ref[units, :])
        sig = jax.nn.sigmoid(pre_gate)
        silu = pre_gate * sig
        hidden = (silu * pre_up).astype(BF)
        gpg = (grad_hidden * pre_up * sig * (1.0 + pre_gate * (1.0 - sig))).astype(BF)
        gpu = (grad_hidden * silu).astype(BF)
        hid_ref[:, units] = hidden
        gpg_ref[:, units] = gpg
        gpu_ref[:, units] = gpu
        hidt_ref[units, :] = hidden.T
        gpgt_ref[units, :] = gpg.T
        gput_ref[units, :] = gpu.T
    hidden = hid_ref[...]
    gpg = gpg_ref[...]
    gpu = gpu_ref[...]
    for j in range(d // cols):
        part = slice(j * cols, (j + 1) * cols)
        out = dot_nn(hidden, wd_ref[:, part])
        grad = dot_nn(gpg, wg_ref[:, part]) + dot_nn(gpu, wu_ref[:, part])
        own = me == j * cols // width
        for at, value in ((j * cols, out), (d + j * cols, grad)):
            near, far = value[: n * ROWS], value[n * ROWS :]
            near, far = jnp.where(own, near, far), jnp.where(own, far, near)
            for b in range(n):
                pairs = ((0, keep_ref, near), (1, send_ref, far))
                if b > 0:
                    pairs = ((0, keep_ref, far), (1, send_ref, near))
                for h, to, rows in pairs:
                    rows = rows[b * ROWS : (b + 1) * ROWS]
                    to[b, :, at : at + cols] = rows[:EIGHT].astype(BF)
                    for x in range(slots - EIGHT):
                        r, c = extra_place(at, x, d)
                        tail_ref[h, b, r : r + 1, c : c + cols] = rows[EIGHT + x : EIGHT + x + 1]
    if slots > EIGHT:
        keep_ref[:, :, 2 * d :] = tail_ref[0].astype(BF)
        send_ref[:, :, 2 * d :] = tail_ref[1].astype(BF)


def grads_kernel(jobs, n, n_old, *refs):
    lefts, rights = refs[:n], refs[n : 2 * n]
    outs, (buf, sems) = refs[2 * n + n_old : 3 * n + n_old], refs[3 * n + n_old :]
    slots = buf.shape[0]
    copies = []
    for i, (a, start, size) in enumerate(jobs):
        slot = i % slots
        if i >= slots:
            copies[i - slots].wait()
        rows = pl.ds(start, size)
        buf[slot, :size] = dot_nn(lefts[a][rows, :], rights[a][...]).astype(BF)
        copy = pltpu.make_async_copy(buf.at[slot, pl.ds(0, size)], outs[a].at[rows, :], sems.at[slot])
        copy.start()
        copies.append(copy)
    for copy in copies[-slots:]:
        copy.wait()


def cores_kernel(keep_ref, got_ref, *out_refs):
    for k, out_ref in enumerate(out_refs):
        out_ref[...] = (keep_ref[k].astype(F32) + got_ref[k].astype(F32)).astype(BF)


def chips_kernel(n, slots, mine_ref, other_ref, *refs):
    ins, outs, total_ref = refs[:n], refs[n:-1], refs[-1]
    tok, width = outs[0].shape
    width //= 2
    d = len(outs) * width
    total = ins[0][...].astype(F32)
    for ref in ins[1:]:
        total = total + ref[...].astype(F32)
    total_ref[...] = total
    first = lax.broadcasted_iota(jnp.int32, (EIGHT, width), 0)
    me = lax.axis_index("expert")

    def rows_at(column):
        rest = jnp.zeros((EIGHT, width), F32)
        for x in range(slots - EIGHT):
            r, c = extra_place(column, x, d)
            row = total_ref[pl.ds(r, 1), lanes_at(2 * d + c, width)]
            rest = jnp.where(first == x, row, rest)
        return jnp.concatenate([total_ref[:, lanes_at(column, width)], rest], axis=0)

    for k, out_ref in enumerate(outs):
        info = other_ref if k else mine_ref
        column = (me ^ k) * width
        rows = jnp.concatenate(
            [(info[:ROWS, :1] * rows_at(column)).astype(BF), rows_at(d + column).astype(BF)], axis=1
        )
        back = info[2 * ROWS : 2 * ROWS + tok, :ROWS].astype(BF)
        out_ref[...] = dot_nn(back, rows).astype(BF)


def home_kernel(*refs):
    ins, (mixed_ref, grad_ref) = refs[:-2], refs[-2:]
    width = mixed_ref.shape[1]
    total = ins[0][...].astype(F32)
    for ref in ins[1:]:
        total = total + ref[...].astype(F32)
    mixed_ref[...] = total[:, :width].astype(BF)
    grad_ref[...] = total[:, width:].astype(BF)


def grads(jobs, lefts, rights, old):
    n = len(lefts)
    f, rows = lefts[0].shape
    d = rights[0].shape[1]
    kept = [a for a in range(n) if old[a] is not None]
    size = max(job[2] for job in jobs)
    done = sum(job[2] for job in jobs)
    return pl.pallas_call(
        functools.partial(grads_kernel, jobs, n, len(kept)),
        in_specs=[VM] * (2 * n) + [HBM] * len(kept),
        out_specs=[HBM] * n,
        out_shape=[jax.ShapeDtypeStruct((f, d), BF)] * n,
        scratch_shapes=[pltpu.VMEM((3, size, d), BF), pltpu.SemaphoreType.DMA((3,))],
        input_output_aliases={2 * n + i: a for i, a in enumerate(kept)},
        compiler_params=params(((6 * size * d + n * 2 * rows * (f + d)) >> 20) + 4),
        cost_estimate=pl.CostEstimate(
            flops=2 * rows * done * d, bytes_accessed=3 * done * d, transcendentals=0
        ),
        name="grads",
    )(*lefts, *rights, *[old[a] for a in kept])


def stack(kernel, arrays, shape, name, scratch=()):
    size = sum(a.size * a.dtype.itemsize for a in arrays)
    return pl.pallas_call(
        kernel,
        in_specs=[VM] * len(arrays),
        out_specs=VM,
        out_shape=jax.ShapeDtypeStruct(shape, BF),
        scratch_shapes=scratch,
        compiler_params=params((size >> 19) + 2),
        name=name,
    )(*arrays)


def per_device(tokens, cotangent, route, gates, w_gate, w_up, w_down):
    n_dp = lax.axis_size("dp")
    n_e = lax.axis_size("expert")
    tok, width = tokens.shape
    d = width * n_e
    f = w_gate.shape[1]
    tile = 256 if f % 256 == 0 else f
    rows = n_dp * ROWS
    n_chip = n_dp // 2
    sds = jax.ShapeDtypeStruct

    def swap(x, chips, experts, core):
        return lax.ppermute(
            x,
            ("dp", "expert"),
            [
                (i * n_e + j, (i ^ (2 * chips + core)) * n_e + (j ^ experts))
                for i in range(n_dp)
                for j in range(n_e)
            ],
        )

    small = n_chip + 4
    slots = min(tok, max(2, 3 * tok // n_e))
    piece = 2 * d // EIGHT
    tail = max(0, slots - EIGHT) * piece
    block_shape = (EIGHT, 2 * d + tail)
    tail_scratch = (EIGHT, max(tail, 128))
    mine = jnp.concatenate([tokens, cotangent], axis=1)[None]
    patterns, hop, first = [0], n_e // 2, True
    while hop:
        patterns = patterns + [p ^ hop for p in patterns]
        got = swap(mine, 0, hop, 1)
        if first:
            info = pl.pallas_call(
                share_kernel,
                in_specs=[VM, VM],
                out_specs=VM,
                out_shape=sds((3 * ROWS, 128), F32),
                compiler_params=params(2),
                cost_estimate=pl.CostEstimate(
                    flops=40 * rows * f * d, bytes_accessed=24 * f * d, transcendentals=0
                ),
                name="share",
            )(route.T, gates.T)
            first = False
            got, info = lax.optimization_barrier((got, info))
            other = swap(info, 0, 0, 1)
        if hop == 1:
            block = stack(
                functools.partial(join_kernel, tuple(patterns), slots),
                [info, other, mine, got],
                block_shape,
                "join",
                [pltpu.VMEM(tail_scratch, F32)],
            )
        else:
            mine = stack(pair_kernel, [mine, got], (len(patterns), tok, 2 * width), "pair")
        hop //= 2
    blocks = [block] + [swap(block, k, 0, 1) for k in range(1, n_chip)]
    near = stack(stack_kernel, blocks, (n_chip,) + block_shape, "stack")
    far = swap(near, 0, 0, 1)

    held = 2 * f * d + rows * (16 * d + 12 * f)
    keep, send, xs, dys, hidden, gpg, gpu = pl.pallas_call(
        functools.partial(expert_kernel, tile=tile, cols=256, slots=slots),
        in_specs=[VM] * 5,
        out_specs=[VM] * 7,
        out_shape=[sds((n_chip,) + block_shape, BF)] * 2
        + [sds((rows, d), BF)] * 2
        + [sds((f, rows), BF)] * 3,
        scratch_shapes=[pltpu.VMEM((rows, f), BF)] * 3
        + [pltpu.VMEM((2, n_chip) + tail_scratch, F32)],
        compiler_params=params((held >> 20) + 4),
        cost_estimate=pl.CostEstimate(
            flops=12 * rows * f * d, bytes_accessed=6 * f * d, transcendentals=rows * f
        ),
        name="expert",
    )(near, far, w_gate[0], w_up[0], w_down[0])

    received = swap(send, 0, 0, 1)
    third, part = f // 3, f // 12
    whole = [(1, i * third, third) for i in range(3)]
    (down,) = grads([(0, 0, 2 * part)], [hidden], [dys], [None])
    received, down = lax.optimization_barrier((received, down))
    parts = pl.pallas_call(
        cores_kernel,
        in_specs=[VM, VM],
        out_specs=[VM] * n_chip,
        out_shape=[sds(block_shape, BF)] * n_chip,
        compiler_params=params(small),
        name="cores",
    )(keep, received)
    arrived = [swap(parts[k], k, 0, 1) for k in range(n_chip - 1, 0, -1)]
    down, grad_gate = grads([(0, 2 * part, 4 * part), (0, 6 * part, 3 * part)] + whole, [hidden, gpg], [dys, xs], [down, None])
    arrived, down, grad_gate = lax.optimization_barrier((arrived, down, grad_gate))
    summed = pl.pallas_call(
        functools.partial(chips_kernel, n_chip, slots),
        in_specs=[VM] * (n_chip + 2),
        out_specs=[VM] * n_e,
        out_shape=[sds((tok, 2 * width), BF)] * n_e,
        scratch_shapes=[pltpu.VMEM(block_shape, F32)],
        compiler_params=params(small),
        name="chips",
    )(info, other, parts[0], *arrived)
    home = [summed[0]] + [swap(summed[k], 0, k, 1) for k in range(n_e - 1, 0, -1)]
    grad_down, grad_up = grads(
        [(0, 9 * part, 3 * part)] + whole, [hidden, gpu], [dys, xs], [down, None]
    )
    home, grad_down, grad_up = lax.optimization_barrier((home, grad_down, grad_up))
    mixed, grad_tokens = pl.pallas_call(
        home_kernel,
        in_specs=[VM] * n_e,
        out_specs=[VM] * 2,
        out_shape=[sds((tok, width), BF)] * 2,
        compiler_params=params(4),
        name="home",
    )(*home)
    return mixed, grad_tokens, grad_gate[None], grad_up[None], grad_down[None]


def solution(mesh):
    return jax.shard_map(
        per_device,
        mesh=mesh,
        in_specs=(
            P("dp", "expert"),
            P("dp", "expert"),
            P("dp", None),
            P("dp", None),
            P("expert", "dp", None),
            P("expert", "dp", None),
            P("expert", "dp", None),
        ),
        out_specs=(
            P("dp", "expert"),
            P("dp", "expert"),
            P("expert", "dp", None),
            P("expert", "dp", None),
            P("expert", "dp", None),
        ),
        check_vma=False,
    )
```

```python
import functools

import jax
import jax.numpy as jnp
from jax import lax
from jax.experimental import pallas as pl
from jax.experimental.pallas import tpu as pltpu
from jax.sharding import PartitionSpec as P

BF = jnp.bfloat16
F32 = jnp.float32
VM = pl.BlockSpec(memory_space=pltpu.VMEM)
HBM = pl.BlockSpec(memory_space=pltpu.HBM)
ROWS = 16
EIGHT = 8


def dot_nn(a, b):
    return lax.dot_general(a, b, (((1,), (0,)), ((), ())), preferred_element_type=F32)


def dot_nt(a, b):
    return lax.dot_general(a, b, (((1,), (1,)), ((), ())), preferred_element_type=F32)


def dot_tn(a, b):
    return lax.dot_general(a, b, (((0,), (0,)), ((), ())), preferred_element_type=F32)


def params(mib):
    return pltpu.CompilerParams(vmem_limit_bytes=mib << 20)


def share_kernel(route_ref, gates_ref, out_ref):
    tok = route_ref.shape[1]
    lanes = out_ref.shape[1]
    hit = route_ref[...] == lax.axis_index("expert")
    routed = jnp.sum(jnp.where(hit, 1.0, 0.0), axis=0, keepdims=True)
    gate = jnp.sum(jnp.where(hit, gates_ref[...], 0.0), axis=0, keepdims=True)
    row = lax.broadcasted_iota(jnp.int32, (tok, tok), 0)
    col = lax.broadcasted_iota(jnp.int32, (tok, tok), 1)
    square = jnp.broadcast_to(routed, (tok, tok))
    routed_col = jnp.sum(jnp.where(row == col, square, 0.0), axis=1, keepdims=True)
    slot_col = jnp.sum(jnp.where(col < row, square, 0.0), axis=1, keepdims=True)
    slot = jnp.sum(jnp.where(row < col, routed_col, 0.0), axis=0, keepdims=True)
    at = lax.broadcasted_iota(jnp.int32, (ROWS, tok), 0).astype(F32)
    pick = jnp.where(at == slot, routed, 0.0)
    weight = jnp.sum(pick * gate, axis=1, keepdims=True)
    out_ref[...] = jnp.zeros_like(out_ref)
    out_ref[:ROWS] = jnp.broadcast_to(weight, (ROWS, lanes))
    out_ref[ROWS : 2 * ROWS, :tok] = pick
    at = lax.broadcasted_iota(jnp.int32, (tok, lanes), 1).astype(F32)
    out_ref[2 * ROWS : 2 * ROWS + tok] = jnp.where(at == slot_col, routed_col, 0.0)


def odd(k):
    return (k ^ (k >> 1) ^ (k >> 2)) & 1


def extra_place(column, extra, d):
    piece = 2 * d // EIGHT
    if isinstance(column, int):
        return column // piece, extra * piece + column % piece
    return lax.div(column, piece), extra * piece + lax.rem(column, piece)


def lanes_at(column, width):
    if not isinstance(column, int):
        column = pl.multiple_of(column, 128)
    return pl.ds(column, width)


def pair_kernel(a_ref, b_ref, out_ref):
    n = a_ref.shape[0]
    out_ref[:n] = a_ref[...]
    out_ref[n:] = b_ref[...]


def join_kernel(patterns, slots, mine_ref, other_ref, a_ref, b_ref, out_ref, tail_ref):
    half, tok, width = a_ref.shape
    width //= 2
    d = len(patterns) * width
    me = lax.axis_index("expert")
    for i, k in enumerate(patterns):
        info = other_ref if odd(k) else mine_ref
        block = a_ref[i] if i < half else b_ref[i - half]
        picked = dot_nn(info[ROWS : 2 * ROWS, :tok].astype(BF), block)
        dys = info[:ROWS, :1] * picked[:, width:]
        for at, rows in ((0, picked[:, :width]), (d, dys)):
            column = at + (me ^ k) * width
            out_ref[:, lanes_at(column, width)] = rows[:EIGHT].astype(BF)
            for x in range(slots - EIGHT):
                r, c = extra_place(column, x, d)
                tail_ref[pl.ds(r, 1), lanes_at(c, width)] = rows[EIGHT + x : EIGHT + x + 1]
    if slots > EIGHT:
        out_ref[:, 2 * d :] = tail_ref[...].astype(BF)


def expert_kernel(*refs, n, tile, cols, slots):
    nears, fars = refs[:n], refs[n : 2 * n]
    (
        wg_ref, wu_ref, wd_ref, keep_ref, send_ref, xs_ref, dys_ref,
        hidt_ref, gpgt_ref, gput_ref,
    hid_ref, gpg_ref, gpu_ref, tail_ref,
    ) = refs[2 * n :]
    f, d = wg_ref.shape
    width = d // lax.axis_size("expert")
    piece = 2 * d // EIGHT
    me = lax.axis_index("expert")
    first = lax.broadcasted_iota(jnp.int32, (EIGHT, width), 0)
    for j in range(d // width):
        for crossed in range(2):

            @pl.when(odd(me ^ j) == crossed)
            def _(j=j, crossed=crossed):
                for b in range(n):
                    near, far = nears[b], fars[b]
                    if crossed ^ (b > 0):
                        near, far = far, near
                    for at, ref in ((b * ROWS, near), ((n + b) * ROWS, far)):
                        for base, to in ((0, xs_ref), (d, dys_ref)):
                            part = slice(j * width, (j + 1) * width)
                            column = base + j * width
                            to[at : at + EIGHT, part] = ref[:, column : column + width]
                            rest = jnp.zeros((EIGHT, width), F32)
                            for x in range(slots - EIGHT):
                                r, c = extra_place(column, x, d)
                                tail = ref[:, 2 * d + c : 2 * d + c + width].astype(F32)
                                rest = jnp.where(first == x, tail[r : r + 1], rest)
                            to[at + EIGHT : at + ROWS, part] = rest.astype(BF)

    xs = xs_ref[...]
    dys = dys_ref[...]
    for i in range(f // tile):
        units = slice(i * tile, (i + 1) * tile)
        pre_gate = dot_nt(xs, wg_ref[units, :])
        pre_up = dot_nt(xs, wu_ref[units, :])
        grad_hidden = dot_nt(dys, wd_ref[units, :])
        sig = jax.nn.sigmoid(pre_gate)
        silu = pre_gate * sig
        hidden = (silu * pre_up).astype(BF)
        gpg = (grad_hidden * pre_up * sig * (1.0 + pre_gate * (1.0 - sig))).astype(BF)
        gpu = (grad_hidden * silu).astype(BF)
        hid_ref[:, units] = hidden
        gpg_ref[:, units] = gpg
        gpu_ref[:, units] = gpu
        hidt_ref[units, :] = hidden.T
        gpgt_ref[units, :] = gpg.T
        gput_ref[units, :] = gpu.T
    hidden = hid_ref[...]
    gpg = gpg_ref[...]
    gpu = gpu_ref[...]
    for j in range(d // cols):
        part = slice(j * cols, (j + 1) * cols)
        out = dot_nn(hidden, wd_ref[:, part])
        grad = dot_nn(gpg, wg_ref[:, part]) + dot_nn(gpu, wu_ref[:, part])
        own = me == j * cols // width
        for at, value in ((j * cols, out), (d + j * cols, grad)):
            near, far = value[: n * ROWS], value[n * ROWS :]
            near, far = jnp.where(own, near, far), jnp.where(own, far, near)
            for b in range(n):
                pairs = ((0, keep_ref, near), (1, send_ref, far))
                if b > 0:
                    pairs = ((0, keep_ref, far), (1, send_ref, near))
                for h, to, rows in pairs:
                    rows = rows[b * ROWS : (b + 1) * ROWS]
                    to[b, :, at : at + cols] = rows[:EIGHT].astype(BF)
                    for x in range(slots - EIGHT):
                        r, c = extra_place(at, x, d)
                        tail_ref[h, b, r : r + 1, c : c + cols] = rows[EIGHT + x : EIGHT + x + 1]
    if slots > EIGHT:
        keep_ref[:, :, 2 * d :] = tail_ref[0].astype(BF)
        send_ref[:, :, 2 * d :] = tail_ref[1].astype(BF)


def grads_kernel(jobs, n, n_old, *refs):
    lefts, rights = refs[:n], refs[n : 2 * n]
    outs, (buf, sems) = refs[2 * n + n_old : 3 * n + n_old], refs[3 * n + n_old :]
    copies = []
    for i, (a, start, size) in enumerate(jobs):
        rows = pl.ds(start, size)
        buf[i, :size] = dot_nn(lefts[a][rows, :], rights[a][...]).astype(BF)
        copy = pltpu.make_async_copy(buf.at[i, pl.ds(0, size)], outs[a].at[rows, :], sems.at[i])
        copy.start()
        copies.append(copy)
    for copy in copies:
        copy.wait()


def cores_kernel(keep_ref, got_ref, *out_refs):
    for k, out_ref in enumerate(out_refs):
        out_ref[...] = (keep_ref[k].astype(F32) + got_ref[k].astype(F32)).astype(BF)


def chips_kernel(n, slots, mine_ref, other_ref, *refs):
    ins, outs, total_ref = refs[:n], refs[n:-1], refs[-1]
    tok, width = outs[0].shape
    width //= 2
    d = len(outs) * width
    total = ins[0][...].astype(F32)
    for ref in ins[1:]:
        total = total + ref[...].astype(F32)
    total_ref[...] = total
    first = lax.broadcasted_iota(jnp.int32, (EIGHT, width), 0)
    me = lax.axis_index("expert")

    def rows_at(column):
        rest = jnp.zeros((EIGHT, width), F32)
        for x in range(slots - EIGHT):
            r, c = extra_place(column, x, d)
            row = total_ref[pl.ds(r, 1), lanes_at(2 * d + c, width)]
            rest = jnp.where(first == x, row, rest)
        return jnp.concatenate([total_ref[:, lanes_at(column, width)], rest], axis=0)

    for k, out_ref in enumerate(outs):
        info = other_ref if k else mine_ref
        column = (me ^ k) * width
        rows = jnp.concatenate(
            [(info[:ROWS, :1] * rows_at(column)).astype(BF), rows_at(d + column).astype(BF)], axis=1
        )
        back = info[2 * ROWS : 2 * ROWS + tok, :ROWS].astype(BF)
        out_ref[...] = dot_nn(back, rows).astype(BF)


def home_kernel(*refs):
    ins, (mixed_ref, grad_ref) = refs[:-2], refs[-2:]
    width = mixed_ref.shape[1]
    total = ins[0][...].astype(F32)
    for ref in ins[1:]:
        total = total + ref[...].astype(F32)
    mixed_ref[...] = total[:, :width].astype(BF)
    grad_ref[...] = total[:, width:].astype(BF)


def grads(spans, lefts, rights, old):
    n = len(lefts)
    f, rows = lefts[0].shape
    d = rights[0].shape[1]
    kept = [a for a in range(n) if old[a] is not None]
    size = f // 12
    jobs = [
        (a, at, min(size, stop - at)) for a, start, stop in spans for at in range(start, stop, size)
    ]
    done = sum(job[2] for job in jobs)
    return pl.pallas_call(
        functools.partial(grads_kernel, jobs, n, len(kept)),
        in_specs=[VM] * (2 * n) + [HBM] * len(kept),
        out_specs=[HBM] * n,
        out_shape=[jax.ShapeDtypeStruct((f, d), BF)] * n,
        scratch_shapes=[
            pltpu.VMEM((len(jobs), size, d), BF),
            pltpu.SemaphoreType.DMA((len(jobs),)),
        ],
        input_output_aliases={2 * n + i: a for i, a in enumerate(kept)},
        compiler_params=params(((2 * len(jobs) * size * d + n * 2 * rows * (f + d)) >> 20) + 4),
        cost_estimate=pl.CostEstimate(
            flops=2 * rows * done * d, bytes_accessed=3 * done * d, transcendentals=0
        ),
        name="grads",
    )(*lefts, *rights, *[old[a] for a in kept])


def stack(kernel, arrays, shape, name, scratch=()):
    size = sum(a.size * a.dtype.itemsize for a in arrays)
    return pl.pallas_call(
        kernel,
        in_specs=[VM] * len(arrays),
        out_specs=VM,
        out_shape=jax.ShapeDtypeStruct(shape, BF),
        scratch_shapes=scratch,
        compiler_params=params((size >> 19) + 2),
        name=name,
    )(*arrays)


def per_device(tokens, cotangent, route, gates, w_gate, w_up, w_down):
    n_dp = lax.axis_size("dp")
    n_e = lax.axis_size("expert")
    tok, width = tokens.shape
    d = width * n_e
    f = w_gate.shape[1]
    tile = 384 if f % 384 == 0 else f
    rows = n_dp * ROWS
    n_chip = n_dp // 2
    sds = jax.ShapeDtypeStruct

    def swap(x, chips, experts, core):
        return lax.ppermute(
            x,
            ("dp", "expert"),
            [
                (i * n_e + j, (i ^ (2 * chips + core)) * n_e + (j ^ experts))
                for i in range(n_dp)
                for j in range(n_e)
            ],
        )

    small = n_chip + 4
    slots = min(tok, max(2, 3 * tok // n_e))
    piece = 2 * d // EIGHT
    tail = max(0, slots - EIGHT) * piece
    block_shape = (EIGHT, 2 * d + tail)
    tail_scratch = (EIGHT, max(tail, 128))
    mine = jnp.concatenate([tokens, cotangent], axis=1)[None]
    patterns, hop, first = [0], n_e // 2, True
    while hop:
        patterns = patterns + [p ^ hop for p in patterns]
        got = swap(mine, 0, hop, 1)
        if first:
            info = pl.pallas_call(
                share_kernel,
                in_specs=[VM, VM],
                out_specs=VM,
                out_shape=sds((3 * ROWS, 128), F32),
                compiler_params=params(2),
                cost_estimate=pl.CostEstimate(
                    flops=40 * rows * f * d, bytes_accessed=24 * f * d, transcendentals=0
                ),
                name="share",
            )(route.T, gates.T)
            first = False
            got, info = lax.optimization_barrier((got, info))
            other = swap(info, 0, 0, 1)
        if hop == 1:
            block = stack(
                functools.partial(join_kernel, tuple(patterns), slots),
                [info, other, mine, got],
                block_shape,
                "join",
                [pltpu.VMEM(tail_scratch, F32)],
            )
        else:
            mine = stack(pair_kernel, [mine, got], (len(patterns), tok, 2 * width), "pair")
        hop //= 2
    blocks = [block] + [swap(block, k, 0, 1) for k in range(1, n_chip)]
    blocks = blocks + [swap(b, 0, 0, 1) for b in blocks]

    held = 2 * f * d + rows * (16 * d + 12 * f)
    keep, send, xs, dys, hidden, gpg, gpu = pl.pallas_call(
        functools.partial(expert_kernel, n=n_chip, tile=tile, cols=256, slots=slots),
        in_specs=[VM] * (2 * n_chip + 3),
        out_specs=[VM] * 7,
        out_shape=[sds((n_chip,) + block_shape, BF)] * 2
        + [sds((rows, d), BF)] * 2
        + [sds((f, rows), BF)] * 3,
        scratch_shapes=[pltpu.VMEM((rows, f), BF)] * 3
        + [pltpu.VMEM((2, n_chip) + tail_scratch, F32)],
        compiler_params=params((held >> 20) + 4),
        cost_estimate=pl.CostEstimate(
            flops=12 * rows * f * d, bytes_accessed=6 * f * d, transcendentals=rows * f
        ),
        name="expert",
    )(*blocks, w_gate[0], w_up[0], w_down[0])

    received = swap(send, 0, 0, 1)
    part = f // 24
    (down,) = grads([(0, 0, 6 * part)], [hidden], [dys], [None])
    received, down = lax.optimization_barrier((received, down))
    parts = pl.pallas_call(
        cores_kernel,
        in_specs=[VM, VM],
        out_specs=[VM] * n_chip,
        out_shape=[sds(block_shape, BF)] * n_chip,
        compiler_params=params(small),
        name="cores",
    )(keep, received)
    arrived = [swap(parts[k], k, 0, 1) for k in range(n_chip - 1, 0, -1)]
    down, grad_gate = grads([(0, 6 * part, 18 * part), (1, 0, f)], [hidden, gpg], [dys, xs], [down, None])
    arrived, down, grad_gate = lax.optimization_barrier((arrived, down, grad_gate))
    summed = pl.pallas_call(
        functools.partial(chips_kernel, n_chip, slots),
        in_specs=[VM] * (n_chip + 2),
        out_specs=[VM] * n_e,
        out_shape=[sds((tok, 2 * width), BF)] * n_e,
        scratch_shapes=[pltpu.VMEM(block_shape, F32)],
        compiler_params=params(small),
        name="chips",
    )(info, other, parts[0], *arrived)
    home = [summed[0]] + [swap(summed[k], 0, k, 1) for k in range(n_e - 1, 0, -1)]
    grad_down, grad_up = grads(
        [(0, 18 * part, f), (1, 0, f)], [hidden, gpu], [dys, xs], [down, None]
    )
    home, grad_down, grad_up = lax.optimization_barrier((home, grad_down, grad_up))
    mixed, grad_tokens = pl.pallas_call(
        home_kernel,
        in_specs=[VM] * n_e,
        out_specs=[VM] * 2,
        out_shape=[sds((tok, width), BF)] * 2,
        compiler_params=params(4),
        name="home",
    )(*home)
    return mixed, grad_tokens, grad_gate[None], grad_up[None], grad_down[None]


def solution(mesh):
    return jax.shard_map(
        per_device,
        mesh=mesh,
        in_specs=(
            P("dp", "expert"),
            P("dp", "expert"),
            P("dp", None),
            P("dp", None),
            P("expert", "dp", None),
            P("expert", "dp", None),
            P("expert", "dp", None),
        ),
        out_specs=(
            P("dp", "expert"),
            P("dp", "expert"),
            P("expert", "dp", None),
            P("expert", "dp", None),
            P("expert", "dp", None),
        ),
        check_vma=False,
    )
```

```python
import functools

import jax
import jax.numpy as jnp
from jax import lax
from jax.experimental import pallas as pl
from jax.experimental.pallas import tpu as pltpu
from jax.sharding import PartitionSpec as P

BF = jnp.bfloat16
F32 = jnp.float32
VM = pl.BlockSpec(memory_space=pltpu.VMEM)
HBM = pl.BlockSpec(memory_space=pltpu.HBM)
ROWS = 16
EIGHT = 8


def dot_nn(a, b):
    return lax.dot_general(a, b, (((1,), (0,)), ((), ())), preferred_element_type=F32)


def dot_nt(a, b):
    return lax.dot_general(a, b, (((1,), (1,)), ((), ())), preferred_element_type=F32)


def dot_tn(a, b):
    return lax.dot_general(a, b, (((0,), (0,)), ((), ())), preferred_element_type=F32)


def params(mib):
    return pltpu.CompilerParams(vmem_limit_bytes=mib << 20)


def share_kernel(route_ref, gates_ref, out_ref):
    tok = route_ref.shape[1]
    lanes = out_ref.shape[1]
    hit = route_ref[...] == lax.axis_index("expert")
    routed = jnp.sum(jnp.where(hit, 1.0, 0.0), axis=0, keepdims=True)
    gate = jnp.sum(jnp.where(hit, gates_ref[...], 0.0), axis=0, keepdims=True)
    row = lax.broadcasted_iota(jnp.int32, (tok, tok), 0)
    col = lax.broadcasted_iota(jnp.int32, (tok, tok), 1)
    square = jnp.broadcast_to(routed, (tok, tok))
    routed_col = jnp.sum(jnp.where(row == col, square, 0.0), axis=1, keepdims=True)
    slot_col = jnp.sum(jnp.where(col < row, square, 0.0), axis=1, keepdims=True)
    slot = jnp.sum(jnp.where(row < col, routed_col, 0.0), axis=0, keepdims=True)
    at = lax.broadcasted_iota(jnp.int32, (ROWS, tok), 0).astype(F32)
    pick = jnp.where(at == slot, routed, 0.0)
    weight = jnp.sum(pick * gate, axis=1, keepdims=True)
    at = lax.broadcasted_iota(jnp.int32, (tok, ROWS), 1).astype(F32)
    back = jnp.where(at == slot_col, routed_col, 0.0)
    out_ref[:ROWS] = jnp.broadcast_to(weight, (ROWS, lanes))
    for i in range(2):
        out_ref[ROWS * (1 + i) : ROWS * (2 + i)] = dot_nn(pick, shifted((tok, lanes), tok * i))
    total = jnp.zeros((2 * tok, lanes), F32)
    for i in range(2):
        wide = dot_nn(back, shifted((ROWS, lanes), ROWS * i))
        total = total + dot_nn(shifted((2 * tok, tok), -tok * i), wide)
    out_ref[3 * ROWS :] = total


def shifted(shape, by):
    row = lax.broadcasted_iota(jnp.int32, shape, 0)
    return jnp.where(row + by == lax.broadcasted_iota(jnp.int32, shape, 1), 1.0, 0.0)


def odd(k):
    return (k ^ (k >> 1) ^ (k >> 2)) & 1


def extra_place(column, extra, d):
    piece = 2 * d // EIGHT
    if isinstance(column, int):
        return column // piece, extra * piece + column % piece
    return lax.div(column, piece), extra * piece + lax.rem(column, piece)


def lanes_at(column, width):
    if not isinstance(column, int):
        column = pl.multiple_of(column, 128)
    return pl.ds(column, width)


def pair_kernel(a_ref, b_ref, out_ref):
    n = a_ref.shape[0]
    out_ref[:n] = a_ref[...]
    out_ref[n:] = b_ref[...]


def join_kernel(patterns, slots, mine_ref, other_ref, a_ref, b_ref, out_ref, tail_ref):
    half, pair, width = a_ref.shape
    d = len(patterns) * width
    me = lax.axis_index("expert")
    for i, k in enumerate(patterns):
        info = other_ref if odd(k) else mine_ref
        block = a_ref[i] if i < half else b_ref[i - half]
        picked = dot_nn(info[ROWS : 3 * ROWS, :pair].astype(BF), block)
        dys = info[:ROWS, :1] * picked[ROWS:]
        for at, rows in ((0, picked[:ROWS]), (d, dys)):
            column = at + (me ^ k) * width
            out_ref[:, lanes_at(column, width)] = rows[:EIGHT].astype(BF)
            for x in range(slots - EIGHT):
                r, c = extra_place(column, x, d)
                tail_ref[pl.ds(r, 1), lanes_at(c, width)] = rows[EIGHT + x : EIGHT + x + 1]
    if slots > EIGHT:
        out_ref[:, 2 * d :] = tail_ref[...].astype(BF)


def expert_kernel(*refs, n, tile, cols, slots):
    nears, fars = refs[:n], refs[n : 2 * n]
    (
        wg_ref, wu_ref, wd_ref, keep_ref, send_ref, xs_ref, dys_ref,
        hidt_ref, gpgt_ref, gput_ref,
    hid_ref, gpg_ref, gpu_ref, tail_ref,
    ) = refs[2 * n :]
    f, d = wg_ref.shape
    width = d // lax.axis_size("expert")
    piece = 2 * d // EIGHT
    me = lax.axis_index("expert")
    first = lax.broadcasted_iota(jnp.int32, (EIGHT, width), 0)
    for j in range(d // width):
        for crossed in range(2):

            @pl.when(odd(me ^ j) == crossed)
            def _(j=j, crossed=crossed):
                for b in range(n):
                    near, far = nears[b], fars[b]
                    if crossed ^ (b > 0):
                        near, far = far, near
                    for at, ref in ((b * ROWS, near), ((n + b) * ROWS, far)):
                        for base, to in ((0, xs_ref), (d, dys_ref)):
                            part = slice(j * width, (j + 1) * width)
                            column = base + j * width
                            to[at : at + EIGHT, part] = ref[:, column : column + width]
                            rest = jnp.zeros((EIGHT, width), F32)
                            for x in range(slots - EIGHT):
                                r, c = extra_place(column, x, d)
                                tail = ref[:, 2 * d + c : 2 * d + c + width].astype(F32)
                                rest = jnp.where(first == x, tail[r : r + 1], rest)
                            to[at + EIGHT : at + ROWS, part] = rest.astype(BF)

    xs = xs_ref[...]
    dys = dys_ref[...]
    for i in range(f // tile):
        units = slice(i * tile, (i + 1) * tile)
        pre_gate = dot_nt(xs, wg_ref[units, :])
        pre_up = dot_nt(xs, wu_ref[units, :])
        grad_hidden = dot_nt(dys, wd_ref[units, :])
        sig = jax.nn.sigmoid(pre_gate)
        silu = pre_gate * sig
        hidden = (silu * pre_up).astype(BF)
        gpg = (grad_hidden * pre_up * sig * (1.0 + pre_gate * (1.0 - sig))).astype(BF)
        gpu = (grad_hidden * silu).astype(BF)
        hid_ref[:, units] = hidden
        gpg_ref[:, units] = gpg
        gpu_ref[:, units] = gpu
        hidt_ref[units, :] = hidden.T
        gpgt_ref[units, :] = gpg.T
        gput_ref[units, :] = gpu.T
    hidden = hid_ref[...]
    gpg = gpg_ref[...]
    gpu = gpu_ref[...]
    for j in range(d // cols):
        part = slice(j * cols, (j + 1) * cols)
        out = dot_nn(hidden, wd_ref[:, part])
        grad = dot_nn(gpg, wg_ref[:, part]) + dot_nn(gpu, wu_ref[:, part])
        own = me == j * cols // width
        for at, value in ((j * cols, out), (d + j * cols, grad)):
            near, far = value[: n * ROWS], value[n * ROWS :]
            near, far = jnp.where(own, near, far), jnp.where(own, far, near)
            for b in range(n):
                pairs = ((0, keep_ref, near), (1, send_ref, far))
                if b > 0:
                    pairs = ((0, keep_ref, far), (1, send_ref, near))
                for h, to, rows in pairs:
                    rows = rows[b * ROWS : (b + 1) * ROWS]
                    to[b, :, at : at + cols] = rows[:EIGHT].astype(BF)
                    for x in range(slots - EIGHT):
                        r, c = extra_place(at, x, d)
                        tail_ref[h, b, r : r + 1, c : c + cols] = rows[EIGHT + x : EIGHT + x + 1]
    if slots > EIGHT:
        keep_ref[:, :, 2 * d :] = tail_ref[0].astype(BF)
        send_ref[:, :, 2 * d :] = tail_ref[1].astype(BF)


def grads_kernel(jobs, n, n_old, *refs):
    lefts, rights = refs[:n], refs[n : 2 * n]
    outs, (buf, sems) = refs[2 * n + n_old : 3 * n + n_old], refs[3 * n + n_old :]
    copies = []
    for i, (a, start, size) in enumerate(jobs):
        rows = pl.ds(start, size)
        buf[i, :size] = dot_nn(lefts[a][rows, :], rights[a][...]).astype(BF)
        copy = pltpu.make_async_copy(buf.at[i, pl.ds(0, size)], outs[a].at[rows, :], sems.at[i])
        copy.start()
        copies.append(copy)
    for copy in copies:
        copy.wait()


def cores_kernel(keep_ref, got_ref, *out_refs):
    for k, out_ref in enumerate(out_refs):
        out_ref[...] = (keep_ref[k].astype(F32) + got_ref[k].astype(F32)).astype(BF)


def chips_kernel(n, slots, mine_ref, other_ref, *refs):
    ins, outs, total_ref = refs[:n], refs[n:-1], refs[-1]
    width = outs[0].shape[1]
    d = len(outs) * width
    total = ins[0][...].astype(F32)
    for ref in ins[1:]:
        total = total + ref[...].astype(F32)
    total_ref[...] = total
    first = lax.broadcasted_iota(jnp.int32, (EIGHT, width), 0)
    me = lax.axis_index("expert")

    def rows_at(column):
        rest = jnp.zeros((EIGHT, width), F32)
        for x in range(slots - EIGHT):
            r, c = extra_place(column, x, d)
            row = total_ref[pl.ds(r, 1), lanes_at(2 * d + c, width)]
            rest = jnp.where(first == x, row, rest)
        return jnp.concatenate([total_ref[:, lanes_at(column, width)], rest], axis=0)

    for k, out_ref in enumerate(outs):
        info = other_ref if k else mine_ref
        column = (me ^ k) * width
        rows = jnp.concatenate(
            [(info[:ROWS, :1] * rows_at(column)).astype(BF), rows_at(d + column).astype(BF)], axis=0
        )
        back = info[3 * ROWS :, : 2 * ROWS].astype(BF)
        out_ref[...] = dot_nn(back, rows).astype(BF)


def home_kernel(*refs):
    ins, (mixed_ref, grad_ref) = refs[:-2], refs[-2:]
    tok = mixed_ref.shape[0]
    total = ins[0][...].astype(F32)
    for ref in ins[1:]:
        total = total + ref[...].astype(F32)
    mixed_ref[...] = total[:tok].astype(BF)
    grad_ref[...] = total[tok:].astype(BF)


def grads(spans, lefts, rights, old):
    n = len(lefts)
    f, rows = lefts[0].shape
    d = rights[0].shape[1]
    kept = [a for a in range(n) if old[a] is not None]
    size = f // 12
    jobs = [
        (a, at, min(size, stop - at)) for a, start, stop in spans for at in range(start, stop, size)
    ]
    done = sum(job[2] for job in jobs)
    return pl.pallas_call(
        functools.partial(grads_kernel, jobs, n, len(kept)),
        in_specs=[VM] * (2 * n) + [HBM] * len(kept),
        out_specs=[HBM] * n,
        out_shape=[jax.ShapeDtypeStruct((f, d), BF)] * n,
        scratch_shapes=[
            pltpu.VMEM((len(jobs), size, d), BF),
            pltpu.SemaphoreType.DMA((len(jobs),)),
        ],
        input_output_aliases={2 * n + i: a for i, a in enumerate(kept)},
        compiler_params=params(((2 * len(jobs) * size * d + n * 2 * rows * (f + d)) >> 20) + 4),
        cost_estimate=pl.CostEstimate(
            flops=2 * rows * done * d, bytes_accessed=3 * done * d, transcendentals=0
        ),
        name="grads",
    )(*lefts, *rights, *[old[a] for a in kept])


def stack(kernel, arrays, shape, name, scratch=()):
    size = sum(a.size * a.dtype.itemsize for a in arrays)
    return pl.pallas_call(
        kernel,
        in_specs=[VM] * len(arrays),
        out_specs=VM,
        out_shape=jax.ShapeDtypeStruct(shape, BF),
        scratch_shapes=scratch,
        compiler_params=params((size >> 19) + 2),
        name=name,
    )(*arrays)


def per_device(tokens, cotangent, route, gates, w_gate, w_up, w_down):
    n_dp = lax.axis_size("dp")
    n_e = lax.axis_size("expert")
    tok, width = tokens.shape
    d = width * n_e
    f = w_gate.shape[1]
    tile = 384 if f % 384 == 0 else f
    rows = n_dp * ROWS
    n_chip = n_dp // 2
    sds = jax.ShapeDtypeStruct

    def swap(x, chips, experts, core):
        return lax.ppermute(
            x,
            ("dp", "expert"),
            [
                (i * n_e + j, (i ^ (2 * chips + core)) * n_e + (j ^ experts))
                for i in range(n_dp)
                for j in range(n_e)
            ],
        )

    small = n_chip + 4
    slots = min(tok, max(2, 3 * tok // n_e))
    piece = 2 * d // EIGHT
    tail = max(0, slots - EIGHT) * piece
    block_shape = (EIGHT, 2 * d + tail)
    tail_scratch = (EIGHT, max(tail, 128))
    mine = jnp.concatenate([tokens, cotangent], axis=0)[None]
    patterns, hop, first = [0], n_e // 2, True
    while hop:
        patterns = patterns + [p ^ hop for p in patterns]
        got = swap(mine, 0, hop, 1)
        if first:
            info = pl.pallas_call(
                share_kernel,
                in_specs=[VM, VM],
                out_specs=VM,
                out_shape=sds((3 * ROWS + 2 * tok, 128), F32),
                compiler_params=params(2),
                cost_estimate=pl.CostEstimate(
                    flops=40 * rows * f * d, bytes_accessed=24 * f * d, transcendentals=0
                ),
                name="share",
            )(route.T, gates.T)
            first = False
            got, info = lax.optimization_barrier((got, info))
            other = swap(info, 0, 0, 1)
        if hop == 1:
            block = stack(
                functools.partial(join_kernel, tuple(patterns), slots),
                [info, other, mine, got],
                block_shape,
                "join",
                [pltpu.VMEM(tail_scratch, F32)],
            )
        else:
            mine = stack(pair_kernel, [mine, got], (len(patterns), 2 * tok, width), "pair")
        hop //= 2
    blocks = [block] + [swap(block, k, 0, 1) for k in range(1, n_chip)]
    blocks = blocks + [swap(b, 0, 0, 1) for b in blocks]

    held = 2 * f * d + rows * (16 * d + 12 * f)
    keep, send, xs, dys, hidden, gpg, gpu = pl.pallas_call(
        functools.partial(expert_kernel, n=n_chip, tile=tile, cols=256, slots=slots),
        in_specs=[VM] * (2 * n_chip + 3),
        out_specs=[VM] * 7,
        out_shape=[sds((n_chip,) + block_shape, BF)] * 2
        + [sds((rows, d), BF)] * 2
        + [sds((f, rows), BF)] * 3,
        scratch_shapes=[pltpu.VMEM((rows, f), BF)] * 3
        + [pltpu.VMEM((2, n_chip) + tail_scratch, F32)],
        compiler_params=params((held >> 20) + 4),
        cost_estimate=pl.CostEstimate(
            flops=12 * rows * f * d, bytes_accessed=6 * f * d, transcendentals=rows * f
        ),
        name="expert",
    )(*blocks, w_gate[0], w_up[0], w_down[0])

    received = swap(send, 0, 0, 1)
    part = f // 24
    (down,) = grads([(0, 0, 6 * part)], [hidden], [dys], [None])
    received, down = lax.optimization_barrier((received, down))
    parts = pl.pallas_call(
        cores_kernel,
        in_specs=[VM, VM],
        out_specs=[VM] * n_chip,
        out_shape=[sds(block_shape, BF)] * n_chip,
        compiler_params=params(small),
        name="cores",
    )(keep, received)
    arrived = [swap(parts[k], k, 0, 1) for k in range(n_chip - 1, 0, -1)]
    down, grad_gate = grads([(0, 6 * part, 18 * part), (1, 0, f)], [hidden, gpg], [dys, xs], [down, None])
    arrived, down, grad_gate = lax.optimization_barrier((arrived, down, grad_gate))
    summed = pl.pallas_call(
        functools.partial(chips_kernel, n_chip, slots),
        in_specs=[VM] * (n_chip + 2),
        out_specs=[VM] * n_e,
        out_shape=[sds((2 * tok, width), BF)] * n_e,
        scratch_shapes=[pltpu.VMEM(block_shape, F32)],
        compiler_params=params(small),
        name="chips",
    )(info, other, parts[0], *arrived)
    home = [summed[0]] + [swap(summed[k], 0, k, 1) for k in range(n_e - 1, 0, -1)]
    grad_down, grad_up = grads(
        [(0, 18 * part, f), (1, 0, f)], [hidden, gpu], [dys, xs], [down, None]
    )
    home, grad_down, grad_up = lax.optimization_barrier((home, grad_down, grad_up))
    mixed, grad_tokens = pl.pallas_call(
        home_kernel,
        in_specs=[VM] * n_e,
        out_specs=[VM] * 2,
        out_shape=[sds((tok, width), BF)] * 2,
        compiler_params=params(4),
        name="home",
    )(*home)
    return mixed, grad_tokens, grad_gate[None], grad_up[None], grad_down[None]


def solution(mesh):
    return jax.shard_map(
        per_device,
        mesh=mesh,
        in_specs=(
            P("dp", "expert"),
            P("dp", "expert"),
            P("dp", None),
            P("dp", None),
            P("expert", "dp", None),
            P("expert", "dp", None),
            P("expert", "dp", None),
        ),
        out_specs=(
            P("dp", "expert"),
            P("dp", "expert"),
            P("expert", "dp", None),
            P("expert", "dp", None),
            P("expert", "dp", None),
        ),
        check_vma=False,
    )
```

```python
import functools

import jax
import jax.numpy as jnp
from jax import lax
from jax.experimental import pallas as pl
from jax.experimental.pallas import tpu as pltpu
from jax.sharding import PartitionSpec as P

BF = jnp.bfloat16
F32 = jnp.float32
VM = pl.BlockSpec(memory_space=pltpu.VMEM)
HBM = pl.BlockSpec(memory_space=pltpu.HBM)
ROWS = 16
EIGHT = 8


def dot_nn(a, b):
    return lax.dot_general(a, b, (((1,), (0,)), ((), ())), preferred_element_type=F32)


def dot_nt(a, b):
    return lax.dot_general(a, b, (((1,), (1,)), ((), ())), preferred_element_type=F32)


def dot_tn(a, b):
    return lax.dot_general(a, b, (((0,), (0,)), ((), ())), preferred_element_type=F32)


def params(mib):
    return pltpu.CompilerParams(vmem_limit_bytes=mib << 20)


def share_kernel(route_ref, gates_ref, out_ref):
    tok = route_ref.shape[1]
    lanes = out_ref.shape[1]
    hit = route_ref[...] == lax.axis_index("expert")
    routed = jnp.sum(jnp.where(hit, 1.0, 0.0), axis=0, keepdims=True)
    gate = jnp.sum(jnp.where(hit, gates_ref[...], 0.0), axis=0, keepdims=True)
    row = lax.broadcasted_iota(jnp.int32, (tok, tok), 0)
    col = lax.broadcasted_iota(jnp.int32, (tok, tok), 1)
    square = jnp.broadcast_to(routed, (tok, tok))
    routed_col = jnp.sum(jnp.where(row == col, square, 0.0), axis=1, keepdims=True)
    slot_col = jnp.sum(jnp.where(col < row, square, 0.0), axis=1, keepdims=True)
    slot = jnp.sum(jnp.where(row < col, routed_col, 0.0), axis=0, keepdims=True)
    at = lax.broadcasted_iota(jnp.int32, (ROWS, tok), 0).astype(F32)
    pick = jnp.where(at == slot, routed, 0.0)
    weight = jnp.sum(pick * gate, axis=1, keepdims=True)
    at = lax.broadcasted_iota(jnp.int32, (tok, ROWS), 1).astype(F32)
    back = jnp.where(at == slot_col, routed_col, 0.0)
    out_ref[:ROWS] = jnp.broadcast_to(weight, (ROWS, lanes))
    for i in range(2):
        out_ref[ROWS * (1 + i) : ROWS * (2 + i)] = dot_nn(pick, shifted((tok, lanes), tok * i))
    total = jnp.zeros((2 * tok, lanes), F32)
    for i in range(2):
        wide = dot_nn(back, shifted((ROWS, lanes), ROWS * i))
        total = total + dot_nn(shifted((2 * tok, tok), -tok * i), wide)
    out_ref[3 * ROWS :] = total


def shifted(shape, by):
    row = lax.broadcasted_iota(jnp.int32, shape, 0)
    return jnp.where(row + by == lax.broadcasted_iota(jnp.int32, shape, 1), 1.0, 0.0)


def odd(k):
    return (k ^ (k >> 1) ^ (k >> 2)) & 1


def extra_place(column, extra, d):
    piece = 2 * d // EIGHT
    if isinstance(column, int):
        return column // piece, extra * piece + column % piece
    return lax.div(column, piece), extra * piece + lax.rem(column, piece)


def lanes_at(column, width):
    if not isinstance(column, int):
        column = pl.multiple_of(column, 128)
    return pl.ds(column, width)


def pair_kernel(a_ref, b_ref, out_ref):
    n = a_ref.shape[0]
    out_ref[:n] = a_ref[...]
    out_ref[n:] = b_ref[...]


def join_kernel(patterns, slots, mine_ref, other_ref, a_ref, b_ref, out_ref, tail_ref):
    half, pair, width = a_ref.shape
    d = len(patterns) * width
    me = lax.axis_index("expert")
    for i, k in enumerate(patterns):
        info = other_ref if odd(k) else mine_ref
        block = a_ref[i] if i < half else b_ref[i - half]
        picked = dot_nn(info[ROWS : 3 * ROWS, :pair].astype(BF), block)
        dys = info[:ROWS, :1] * picked[ROWS:]
        for at, rows in ((0, picked[:ROWS]), (d, dys)):
            column = at + (me ^ k) * width
            out_ref[:, lanes_at(column, width)] = rows[:EIGHT].astype(BF)
            for x in range(slots - EIGHT):
                r, c = extra_place(column, x, d)
                tail_ref[pl.ds(r, 1), lanes_at(c, width)] = rows[EIGHT + x : EIGHT + x + 1]
    if slots > EIGHT:
        out_ref[:, 2 * d :] = tail_ref[...].astype(BF)


def expert_kernel(*refs, n, tile, cols, slots):
    nears, fars = refs[:n], refs[n : 2 * n]
    (
        wg_ref, wu_ref, wd_ref, keep_ref, send_ref, xs_ref, dys_ref,
        hidt_ref, gpgt_ref, gput_ref,
    hid_ref, gpg_ref, gpu_ref, tail_ref,
    ) = refs[2 * n :]
    f, d = wg_ref.shape
    width = d // lax.axis_size("expert")
    piece = 2 * d // EIGHT
    me = lax.axis_index("expert")
    first = lax.broadcasted_iota(jnp.int32, (EIGHT, width), 0)
    for j in range(d // width):
        for crossed in range(2):

            @pl.when(odd(me ^ j) == crossed)
            def _(j=j, crossed=crossed):
                for b in range(n):
                    near, far = nears[b], fars[b]
                    if crossed ^ (b > 0):
                        near, far = far, near
                    for at, ref in ((b * ROWS, near), ((n + b) * ROWS, far)):
                        for base, to in ((0, xs_ref), (d, dys_ref)):
                            part = slice(j * width, (j + 1) * width)
                            column = base + j * width
                            to[at : at + EIGHT, part] = ref[:, column : column + width]
                            rest = jnp.zeros((EIGHT, width), F32)
                            for x in range(slots - EIGHT):
                                r, c = extra_place(column, x, d)
                                tail = ref[:, 2 * d + c : 2 * d + c + width].astype(F32)
                                rest = jnp.where(first == x, tail[r : r + 1], rest)
                            to[at + EIGHT : at + ROWS, part] = rest.astype(BF)

    xs = xs_ref[...]
    dys = dys_ref[...]
    for i in range(f // tile):
        units = slice(i * tile, (i + 1) * tile)
        pre_gate = dot_nt(xs, wg_ref[units, :])
        pre_up = dot_nt(xs, wu_ref[units, :])
        grad_hidden = dot_nt(dys, wd_ref[units, :])
        sig = jax.nn.sigmoid(pre_gate)
        silu = pre_gate * sig
        hidden = (silu * pre_up).astype(BF)
        gpg = (grad_hidden * pre_up * sig * (1.0 + pre_gate * (1.0 - sig))).astype(BF)
        gpu = (grad_hidden * silu).astype(BF)
        hid_ref[:, units] = hidden
        gpg_ref[:, units] = gpg
        gpu_ref[:, units] = gpu
        hidt_ref[units, :] = hidden.T
        gpgt_ref[units, :] = gpg.T
        gput_ref[units, :] = gpu.T
    hidden = hid_ref[...]
    gpg = gpg_ref[...]
    gpu = gpu_ref[...]
    for j in range(d // cols):
        part = slice(j * cols, (j + 1) * cols)
        out = dot_nn(hidden, wd_ref[:, part])
        grad = dot_nn(gpg, wg_ref[:, part]) + dot_nn(gpu, wu_ref[:, part])
        own = me == j * cols // width
        for at, value in ((j * cols, out), (d + j * cols, grad)):
            near, far = value[: n * ROWS], value[n * ROWS :]
            near, far = jnp.where(own, near, far), jnp.where(own, far, near)
            for b in range(n):
                pairs = ((0, keep_ref, near), (1, send_ref, far))
                if b > 0:
                    pairs = ((0, keep_ref, far), (1, send_ref, near))
                for h, to, rows in pairs:
                    rows = rows[b * ROWS : (b + 1) * ROWS]
                    to[b, :, at : at + cols] = rows[:EIGHT].astype(BF)
                    for x in range(slots - EIGHT):
                        r, c = extra_place(at, x, d)
                        tail_ref[h, b, r : r + 1, c : c + cols] = rows[EIGHT + x : EIGHT + x + 1]
    if slots > EIGHT:
        keep_ref[:, :, 2 * d :] = tail_ref[0].astype(BF)
        send_ref[:, :, 2 * d :] = tail_ref[1].astype(BF)


def grads_kernel(jobs, n, n_old, *refs):
    lefts, rights = refs[:n], refs[n : 2 * n]
    outs, (buf, sems) = refs[2 * n + n_old : 3 * n + n_old], refs[3 * n + n_old :]
    copies = []
    for i, (a, start, size) in enumerate(jobs):
        rows = pl.ds(start, size)
        buf[i, :size] = dot_nn(lefts[a][rows, :], rights[a][...]).astype(BF)
        copy = pltpu.make_async_copy(buf.at[i, pl.ds(0, size)], outs[a].at[rows, :], sems.at[i])
        copy.start()
        copies.append(copy)
    for copy in copies:
        copy.wait()


def cores_kernel(keep_ref, got_ref, *out_refs):
    for k, out_ref in enumerate(out_refs):
        out_ref[...] = (keep_ref[k].astype(F32) + got_ref[k].astype(F32)).astype(BF)


def chips_kernel(n, slots, mine_ref, other_ref, *refs):
    ins, outs, total_ref = refs[:n], refs[n:-1], refs[-1]
    width = outs[0].shape[1]
    d = len(outs) * width
    total = ins[0][...].astype(F32)
    for ref in ins[1:]:
        total = total + ref[...].astype(F32)
    total_ref[...] = total
    first = lax.broadcasted_iota(jnp.int32, (EIGHT, width), 0)
    me = lax.axis_index("expert")

    def rows_at(column):
        rest = jnp.zeros((EIGHT, width), F32)
        for x in range(slots - EIGHT):
            r, c = extra_place(column, x, d)
            row = total_ref[pl.ds(r, 1), lanes_at(2 * d + c, width)]
            rest = jnp.where(first == x, row, rest)
        return jnp.concatenate([total_ref[:, lanes_at(column, width)], rest], axis=0)

    for k, out_ref in enumerate(outs):
        info = other_ref if k else mine_ref
        column = (me ^ k) * width
        rows = jnp.concatenate(
            [(info[:ROWS, :1] * rows_at(column)).astype(BF), rows_at(d + column).astype(BF)], axis=0
        )
        back = info[3 * ROWS :, : 2 * ROWS].astype(BF)
        out_ref[...] = dot_nn(back, rows).astype(BF)


def home_kernel(*refs):
    ins, (mixed_ref, grad_ref) = refs[:-2], refs[-2:]
    tok = mixed_ref.shape[0]
    total = ins[0][...].astype(F32)
    for ref in ins[1:]:
        total = total + ref[...].astype(F32)
    mixed_ref[...] = total[:tok].astype(BF)
    grad_ref[...] = total[tok:].astype(BF)


def grads(spans, lefts, rights, old):
    n = len(lefts)
    f, rows = lefts[0].shape
    d = rights[0].shape[1]
    kept = [a for a in range(n) if old[a] is not None]
    size = f // 12
    jobs = [
        (a, at, min(size, stop - at)) for a, start, stop in spans for at in range(start, stop, size)
    ]
    done = sum(job[2] for job in jobs)
    return pl.pallas_call(
        functools.partial(grads_kernel, jobs, n, len(kept)),
        in_specs=[VM] * (2 * n) + [HBM] * len(kept),
        out_specs=[HBM] * n,
        out_shape=[jax.ShapeDtypeStruct((f, d), BF)] * n,
        scratch_shapes=[
            pltpu.VMEM((len(jobs), size, d), BF),
            pltpu.SemaphoreType.DMA((len(jobs),)),
        ],
        input_output_aliases={2 * n + i: a for i, a in enumerate(kept)},
        compiler_params=params(((2 * len(jobs) * size * d + n * 2 * rows * (f + d)) >> 20) + 4),
        cost_estimate=pl.CostEstimate(
            flops=2 * rows * done * d, bytes_accessed=3 * done * d, transcendentals=0
        ),
        name="grads",
    )(*lefts, *rights, *[old[a] for a in kept])


def stack(kernel, arrays, shape, name, scratch=()):
    size = sum(a.size * a.dtype.itemsize for a in arrays)
    return pl.pallas_call(
        kernel,
        in_specs=[VM] * len(arrays),
        out_specs=VM,
        out_shape=jax.ShapeDtypeStruct(shape, BF),
        scratch_shapes=scratch,
        compiler_params=params((size >> 19) + 2),
        name=name,
    )(*arrays)


def per_device(tokens, cotangent, route, gates, w_gate, w_up, w_down):
    n_dp = lax.axis_size("dp")
    n_e = lax.axis_size("expert")
    tok, width = tokens.shape
    d = width * n_e
    f = w_gate.shape[1]
    tile = 384 if f % 384 == 0 else f
    rows = n_dp * ROWS
    n_chip = n_dp // 2
    sds = jax.ShapeDtypeStruct

    def swap(x, chips, experts, core):
        return lax.ppermute(
            x,
            ("dp", "expert"),
            [
                (i * n_e + j, (i ^ (2 * chips + core)) * n_e + (j ^ experts))
                for i in range(n_dp)
                for j in range(n_e)
            ],
        )

    small = n_chip + 4
    slots = min(tok, max(2, 3 * tok // n_e))
    piece = 2 * d // EIGHT
    tail = max(0, slots - EIGHT) * piece
    block_shape = (EIGHT, 2 * d + tail)
    tail_scratch = (EIGHT, max(tail, 128))
    mine = jnp.concatenate([tokens, cotangent], axis=0)[None]
    patterns, hop, first = [0], n_e // 2, True
    while hop:
        patterns = patterns + [p ^ hop for p in patterns]
        got = swap(mine, 0, hop, 1)
        if first:
            info = pl.pallas_call(
                share_kernel,
                in_specs=[VM, VM],
                out_specs=VM,
                out_shape=sds((3 * ROWS + 2 * tok, 128), F32),
                compiler_params=params(2),
                cost_estimate=pl.CostEstimate(
                    flops=40 * rows * f * d, bytes_accessed=24 * f * d, transcendentals=0
                ),
                name="share",
            )(route.T, gates.T)
            first = False
            got, info = lax.optimization_barrier((got, info))
            other = swap(info, 0, 0, 1)
        if hop == 1:
            block = stack(
                functools.partial(join_kernel, tuple(patterns), slots),
                [info, other, mine, got],
                block_shape,
                "join",
                [pltpu.VMEM(tail_scratch, F32)],
            )
        else:
            mine = stack(pair_kernel, [mine, got], (len(patterns), 2 * tok, width), "pair")
        hop //= 2
    blocks = [block] + [swap(block, k, 0, 1) for k in range(1, n_chip)]
    blocks = blocks + [swap(b, 0, 0, 1) for b in blocks]

    held = 2 * f * d + rows * (16 * d + 12 * f)
    keep, send, xs, dys, hidden, gpg, gpu = pl.pallas_call(
        functools.partial(expert_kernel, n=n_chip, tile=tile, cols=256, slots=slots),
        in_specs=[VM] * (2 * n_chip + 3),
        out_specs=[VM] * 7,
        out_shape=[sds((n_chip,) + block_shape, BF)] * 2
        + [sds((rows, d), BF)] * 2
        + [sds((f, rows), BF)] * 3,
        scratch_shapes=[pltpu.VMEM((rows, f), BF)] * 3
        + [pltpu.VMEM((2, n_chip) + tail_scratch, F32)],
        compiler_params=params((held >> 20) + 4),
        cost_estimate=pl.CostEstimate(
            flops=12 * rows * f * d, bytes_accessed=6 * f * d, transcendentals=rows * f
        ),
        name="expert",
    )(*blocks, w_gate[0], w_up[0], w_down[0])

    received = swap(send, 0, 0, 1)
    part = f // 24
    (down,) = grads([(0, 0, 6 * part)], [hidden], [dys], [None])
    received, down = lax.optimization_barrier((received, down))
    parts = pl.pallas_call(
        cores_kernel,
        in_specs=[VM, VM],
        out_specs=[VM] * n_chip,
        out_shape=[sds(block_shape, BF)] * n_chip,
        compiler_params=params(small),
        name="cores",
    )(keep, received)
    arrived = [swap(parts[k], k, 0, 1) for k in range(n_chip - 1, 0, -1)]
    down, grad_gate = grads([(0, 6 * part, 18 * part), (1, 0, f)], [hidden, gpg], [dys, xs], [down, None])
    arrived, down, grad_gate = lax.optimization_barrier((arrived, down, grad_gate))
    summed = pl.pallas_call(
        functools.partial(chips_kernel, n_chip, slots),
        in_specs=[VM] * (n_chip + 2),
        out_specs=[VM] * n_e,
        out_shape=[sds((2 * tok, width), BF)] * n_e,
        scratch_shapes=[pltpu.VMEM(block_shape, F32)],
        compiler_params=params(small),
        name="chips",
    )(info, other, parts[0], *arrived)
    home = [summed[0]] + [
        swap(summed[k], 0, k, 1) for k in sorted(range(1, n_e), key=lambda k: (k != n_e // 2, -k))
    ]
    grad_down, grad_up = grads(
        [(0, 18 * part, f), (1, 0, f)], [hidden, gpu], [dys, xs], [down, None]
    )
    home, grad_down, grad_up = lax.optimization_barrier((home, grad_down, grad_up))
    mixed, grad_tokens = pl.pallas_call(
        home_kernel,
        in_specs=[VM] * n_e,
        out_specs=[VM] * 2,
        out_shape=[sds((tok, width), BF)] * 2,
        compiler_params=params(4),
        name="home",
    )(*home)
    return mixed, grad_tokens, grad_gate[None], grad_up[None], grad_down[None]


def solution(mesh):
    return jax.shard_map(
        per_device,
        mesh=mesh,
        in_specs=(
            P("dp", "expert"),
            P("dp", "expert"),
            P("dp", None),
            P("dp", None),
            P("expert", "dp", None),
            P("expert", "dp", None),
            P("expert", "dp", None),
        ),
        out_specs=(
            P("dp", "expert"),
            P("dp", "expert"),
            P("expert", "dp", None),
            P("expert", "dp", None),
            P("expert", "dp", None),
        ),
        check_vma=False,
    )
```

```python
import functools

import jax
import jax.numpy as jnp
from jax import lax
from jax.experimental import pallas as pl
from jax.experimental.pallas import tpu as pltpu
from jax.sharding import PartitionSpec as P

BF = jnp.bfloat16
F32 = jnp.float32
VM = pl.BlockSpec(memory_space=pltpu.VMEM)
HBM = pl.BlockSpec(memory_space=pltpu.HBM)
ROWS = 16
EIGHT = 8


def dot_nn(a, b):
    return lax.dot_general(a, b, (((1,), (0,)), ((), ())), preferred_element_type=F32)


def dot_nt(a, b):
    return lax.dot_general(a, b, (((1,), (1,)), ((), ())), preferred_element_type=F32)


def dot_tn(a, b):
    return lax.dot_general(a, b, (((0,), (0,)), ((), ())), preferred_element_type=F32)


def params(mib):
    return pltpu.CompilerParams(vmem_limit_bytes=mib << 20)


def share_kernel(route_ref, gates_ref, out_ref):
    tok = route_ref.shape[1]
    lanes = out_ref.shape[1]
    hit = route_ref[...] == lax.axis_index("expert")
    routed = jnp.sum(jnp.where(hit, 1.0, 0.0), axis=0, keepdims=True)
    gate = jnp.sum(jnp.where(hit, gates_ref[...], 0.0), axis=0, keepdims=True)
    row = lax.broadcasted_iota(jnp.int32, (tok, tok), 0)
    col = lax.broadcasted_iota(jnp.int32, (tok, tok), 1)
    square = jnp.broadcast_to(routed, (tok, tok))
    routed_col = jnp.sum(jnp.where(row == col, square, 0.0), axis=1, keepdims=True)
    slot_col = jnp.sum(jnp.where(col < row, square, 0.0), axis=1, keepdims=True)
    slot = jnp.sum(jnp.where(row < col, routed_col, 0.0), axis=0, keepdims=True)
    at = lax.broadcasted_iota(jnp.int32, (ROWS, tok), 0).astype(F32)
    pick = jnp.where(at == slot, routed, 0.0)
    weight = jnp.sum(pick * gate, axis=1, keepdims=True)
    at = lax.broadcasted_iota(jnp.int32, (tok, ROWS), 1).astype(F32)
    back = jnp.where(at == slot_col, routed_col, 0.0)
    out_ref[:ROWS] = jnp.broadcast_to(weight, (ROWS, lanes))
    for i in range(2):
        out_ref[ROWS * (1 + i) : ROWS * (2 + i)] = dot_nn(pick, shifted((tok, lanes), tok * i))
    total = jnp.zeros((2 * tok, lanes), F32)
    for i in range(2):
        wide = dot_nn(back, shifted((ROWS, lanes), ROWS * i))
        total = total + dot_nn(shifted((2 * tok, tok), -tok * i), wide)
    out_ref[3 * ROWS :] = total


def shifted(shape, by):
    row = lax.broadcasted_iota(jnp.int32, shape, 0)
    return jnp.where(row + by == lax.broadcasted_iota(jnp.int32, shape, 1), 1.0, 0.0)


def odd(k):
    return (k ^ (k >> 1) ^ (k >> 2)) & 1


def extra_place(column, extra, d):
    piece = 2 * d // EIGHT
    if isinstance(column, int):
        return column // piece, extra * piece + column % piece
    return lax.div(column, piece), extra * piece + lax.rem(column, piece)


def lanes_at(column, width):
    if not isinstance(column, int):
        column = pl.multiple_of(column, 128)
    return pl.ds(column, width)


def pair_kernel(a_ref, b_ref, out_ref):
    n = a_ref.shape[0]
    out_ref[:n] = a_ref[...]
    out_ref[n:] = b_ref[...]


def join_kernel(patterns, slots, mine_ref, other_ref, a_ref, b_ref, out_ref, tail_ref):
    half, pair, width = a_ref.shape
    d = len(patterns) * width
    me = lax.axis_index("expert")
    for i, k in enumerate(patterns):
        info = other_ref if odd(k) else mine_ref
        block = a_ref[i] if i < half else b_ref[i - half]
        picked = dot_nn(info[ROWS : 3 * ROWS, :pair].astype(BF), block)
        dys = info[:ROWS, :1] * picked[ROWS:]
        for at, rows in ((0, picked[:ROWS]), (d, dys)):
            column = at + (me ^ k) * width
            out_ref[:, lanes_at(column, width)] = rows[:EIGHT].astype(BF)
            for x in range(slots - EIGHT):
                r, c = extra_place(column, x, d)
                tail_ref[pl.ds(r, 1), lanes_at(c, width)] = rows[EIGHT + x : EIGHT + x + 1]
    if slots > EIGHT:
        out_ref[:, 2 * d :] = tail_ref[...].astype(BF)


def expert_kernel(*refs, n, tile, cols, slots):
    nears, fars = refs[:n], refs[n : 2 * n]
    (
        wg_ref, wu_ref, wd_ref, keep_ref, send_ref, xs_ref, dys_ref,
        hidt_ref, gpgt_ref, gput_ref,
    hid_ref, gpg_ref, gpu_ref, tail_ref,
    ) = refs[2 * n :]
    f, d = wg_ref.shape
    width = d // lax.axis_size("expert")
    piece = 2 * d // EIGHT
    me = lax.axis_index("expert")
    first = lax.broadcasted_iota(jnp.int32, (EIGHT, width), 0)
    for j in range(d // width):
        for crossed in range(2):

            @pl.when(odd(me ^ j) == crossed)
            def _(j=j, crossed=crossed):
                for b in range(n):
                    near, far = nears[b], fars[b]
                    if crossed ^ (b > 0):
                        near, far = far, near
                    for at, ref in ((b * ROWS, near), ((n + b) * ROWS, far)):
                        for base, to in ((0, xs_ref), (d, dys_ref)):
                            part = slice(j * width, (j + 1) * width)
                            column = base + j * width
                            to[at : at + EIGHT, part] = ref[:, column : column + width]
                            rest = jnp.zeros((EIGHT, width), F32)
                            for x in range(slots - EIGHT):
                                r, c = extra_place(column, x, d)
                                tail = ref[:, 2 * d + c : 2 * d + c + width].astype(F32)
                                rest = jnp.where(first == x, tail[r : r + 1], rest)
                            to[at + EIGHT : at + ROWS, part] = rest.astype(BF)

    xs = xs_ref[...]
    dys = dys_ref[...]
    for i in range(f // tile):
        units = slice(i * tile, (i + 1) * tile)
        pre_gate = dot_nt(xs, wg_ref[units, :])
        pre_up = dot_nt(xs, wu_ref[units, :])
        grad_hidden = dot_nt(dys, wd_ref[units, :])
        sig = jax.nn.sigmoid(pre_gate)
        silu = pre_gate * sig
        hidden = (silu * pre_up).astype(BF)
        gpg = (grad_hidden * pre_up * sig * (1.0 + pre_gate * (1.0 - sig))).astype(BF)
        gpu = (grad_hidden * silu).astype(BF)
        hid_ref[:, units] = hidden
        gpg_ref[:, units] = gpg
        gpu_ref[:, units] = gpu
        hidt_ref[units, :] = hidden.T
        gpgt_ref[units, :] = gpg.T
        gput_ref[units, :] = gpu.T
    hidden = hid_ref[...]
    gpg = gpg_ref[...]
    gpu = gpu_ref[...]
    for j in range(d // cols):
        part = slice(j * cols, (j + 1) * cols)
        out = dot_nn(hidden, wd_ref[:, part])
        grad = dot_nn(gpg, wg_ref[:, part]) + dot_nn(gpu, wu_ref[:, part])
        own = me == j * cols // width
        for at, value in ((j * cols, out), (d + j * cols, grad)):
            near, far = value[: n * ROWS], value[n * ROWS :]
            near, far = jnp.where(own, near, far), jnp.where(own, far, near)
            for b in range(n):
                pairs = ((0, keep_ref, near), (1, send_ref, far))
                if b > 0:
                    pairs = ((0, keep_ref, far), (1, send_ref, near))
                for h, to, rows in pairs:
                    rows = rows[b * ROWS : (b + 1) * ROWS]
                    to[b, :, at : at + cols] = rows[:EIGHT].astype(BF)
                    for x in range(slots - EIGHT):
                        r, c = extra_place(at, x, d)
                        tail_ref[h, b, r : r + 1, c : c + cols] = rows[EIGHT + x : EIGHT + x + 1]
    if slots > EIGHT:
        keep_ref[:, :, 2 * d :] = tail_ref[0].astype(BF)
        send_ref[:, :, 2 * d :] = tail_ref[1].astype(BF)


def grads_kernel(jobs, n, n_old, *refs):
    lefts, rights = refs[:n], refs[n : 2 * n]
    outs, (buf, sems) = refs[2 * n + n_old : 3 * n + n_old], refs[3 * n + n_old :]
    copies = []
    for i, (a, start, size) in enumerate(jobs):
        rows = pl.ds(start, size)
        buf[i, :size] = dot_nn(lefts[a][rows, :], rights[a][...]).astype(BF)
        copy = pltpu.make_async_copy(buf.at[i, pl.ds(0, size)], outs[a].at[rows, :], sems.at[i])
        copy.start()
        copies.append(copy)
    for copy in copies:
        copy.wait()


def cores_kernel(keep_ref, got_ref, *out_refs):
    for k, out_ref in enumerate(out_refs):
        out_ref[...] = (keep_ref[k].astype(F32) + got_ref[k].astype(F32)).astype(BF)


def chips_kernel(n, slots, mine_ref, other_ref, *refs):
    ins, outs, total_ref = refs[:n], refs[n:-1], refs[-1]
    width = outs[0].shape[1]
    d = len(outs) * width
    total = ins[0][...].astype(F32)
    for ref in ins[1:]:
        total = total + ref[...].astype(F32)
    total_ref[...] = total
    first = lax.broadcasted_iota(jnp.int32, (EIGHT, width), 0)
    me = lax.axis_index("expert")

    def rows_at(column):
        rest = jnp.zeros((EIGHT, width), F32)
        for x in range(slots - EIGHT):
            r, c = extra_place(column, x, d)
            row = total_ref[pl.ds(r, 1), lanes_at(2 * d + c, width)]
            rest = jnp.where(first == x, row, rest)
        return jnp.concatenate([total_ref[:, lanes_at(column, width)], rest], axis=0)

    for k, out_ref in enumerate(outs):
        info = other_ref if k else mine_ref
        column = (me ^ k) * width
        rows = jnp.concatenate(
            [(info[:ROWS, :1] * rows_at(column)).astype(BF), rows_at(d + column).astype(BF)], axis=0
        )
        back = info[3 * ROWS :, : 2 * ROWS].astype(BF)
        out_ref[...] = dot_nn(back, rows).astype(BF)


def home_kernel(*refs):
    ins, (mixed_ref, grad_ref) = refs[:-2], refs[-2:]
    tok = mixed_ref.shape[0]
    total = ins[0][...].astype(F32)
    for ref in ins[1:]:
        total = total + ref[...].astype(F32)
    mixed_ref[...] = total[:tok].astype(BF)
    grad_ref[...] = total[tok:].astype(BF)


def grads(spans, lefts, rights, old):
    n = len(lefts)
    f, rows = lefts[0].shape
    d = rights[0].shape[1]
    kept = [a for a in range(n) if old[a] is not None]
    size = f // (24 if n == 1 else 12)
    jobs = [
        (a, at, min(size, stop - at)) for a, start, stop in spans for at in range(start, stop, size)
    ]
    done = sum(job[2] for job in jobs)
    return pl.pallas_call(
        functools.partial(grads_kernel, jobs, n, len(kept)),
        in_specs=[VM] * (2 * n) + [HBM] * len(kept),
        out_specs=[HBM] * n,
        out_shape=[jax.ShapeDtypeStruct((f, d), BF)] * n,
        scratch_shapes=[
            pltpu.VMEM((len(jobs), size, d), BF),
            pltpu.SemaphoreType.DMA((len(jobs),)),
        ],
        input_output_aliases={2 * n + i: a for i, a in enumerate(kept)},
        compiler_params=params(((2 * len(jobs) * size * d + n * 2 * rows * (f + d)) >> 20) + 4),
        cost_estimate=pl.CostEstimate(
            flops=2 * rows * done * d, bytes_accessed=3 * done * d, transcendentals=0
        ),
        name="grads",
    )(*lefts, *rights, *[old[a] for a in kept])


def stack(kernel, arrays, shape, name, scratch=()):
    size = sum(a.size * a.dtype.itemsize for a in arrays)
    return pl.pallas_call(
        kernel,
        in_specs=[VM] * len(arrays),
        out_specs=VM,
        out_shape=jax.ShapeDtypeStruct(shape, BF),
        scratch_shapes=scratch,
        compiler_params=params((size >> 19) + 2),
        name=name,
    )(*arrays)


def per_device(tokens, cotangent, route, gates, w_gate, w_up, w_down):
    n_dp = lax.axis_size("dp")
    n_e = lax.axis_size("expert")
    tok, width = tokens.shape
    d = width * n_e
    f = w_gate.shape[1]
    tile = 384 if f % 384 == 0 else f
    rows = n_dp * ROWS
    n_chip = n_dp // 2
    sds = jax.ShapeDtypeStruct

    def swap(x, chips, experts, core):
        return lax.ppermute(
            x,
            ("dp", "expert"),
            [
                (i * n_e + j, (i ^ (2 * chips + core)) * n_e + (j ^ experts))
                for i in range(n_dp)
                for j in range(n_e)
            ],
        )

    small = n_chip + 4
    slots = min(tok, max(2, 3 * tok // n_e))
    piece = 2 * d // EIGHT
    tail = max(0, slots - EIGHT) * piece
    block_shape = (EIGHT, 2 * d + tail)
    tail_scratch = (EIGHT, max(tail, 128))
    mine = jnp.concatenate([tokens, cotangent], axis=0)[None]
    patterns, hop, first = [0], n_e // 2, True
    while hop:
        patterns = patterns + [p ^ hop for p in patterns]
        got = swap(mine, 0, hop, 1)
        if first:
            info = pl.pallas_call(
                share_kernel,
                in_specs=[VM, VM],
                out_specs=VM,
                out_shape=sds((3 * ROWS + 2 * tok, 128), F32),
                compiler_params=params(2),
                cost_estimate=pl.CostEstimate(
                    flops=40 * rows * f * d, bytes_accessed=24 * f * d, transcendentals=0
                ),
                name="share",
            )(route.T, gates.T)
            first = False
            got, info = lax.optimization_barrier((got, info))
            other = swap(info, 0, 0, 1)
        if hop == 1:
            block = stack(
                functools.partial(join_kernel, tuple(patterns), slots),
                [info, other, mine, got],
                block_shape,
                "join",
                [pltpu.VMEM(tail_scratch, F32)],
            )
        else:
            mine = stack(pair_kernel, [mine, got], (len(patterns), 2 * tok, width), "pair")
        hop //= 2
    blocks = [block] + [swap(block, k, 0, 1) for k in range(1, n_chip)]
    blocks = blocks + [swap(b, 0, 0, 1) for b in blocks]

    held = 2 * f * d + rows * (16 * d + 12 * f)
    keep, send, xs, dys, hidden, gpg, gpu = pl.pallas_call(
        functools.partial(expert_kernel, n=n_chip, tile=tile, cols=256, slots=slots),
        in_specs=[VM] * (2 * n_chip + 3),
        out_specs=[VM] * 7,
        out_shape=[sds((n_chip,) + block_shape, BF)] * 2
        + [sds((rows, d), BF)] * 2
        + [sds((f, rows), BF)] * 3,
        scratch_shapes=[pltpu.VMEM((rows, f), BF)] * 3
        + [pltpu.VMEM((2, n_chip) + tail_scratch, F32)],
        compiler_params=params((held >> 20) + 4),
        cost_estimate=pl.CostEstimate(
            flops=12 * rows * f * d, bytes_accessed=6 * f * d, transcendentals=rows * f
        ),
        name="expert",
    )(*blocks, w_gate[0], w_up[0], w_down[0])

    received = swap(send, 0, 0, 1)
    part = f // 24
    (down,) = grads([(0, 0, 6 * part)], [hidden], [dys], [None])
    received, down = lax.optimization_barrier((received, down))
    parts = pl.pallas_call(
        cores_kernel,
        in_specs=[VM, VM],
        out_specs=[VM] * n_chip,
        out_shape=[sds(block_shape, BF)] * n_chip,
        compiler_params=params(small),
        name="cores",
    )(keep, received)
    arrived = [swap(parts[k], k, 0, 1) for k in range(n_chip - 1, 0, -1)]
    down, grad_gate = grads([(0, 6 * part, 18 * part), (1, 0, f)], [hidden, gpg], [dys, xs], [down, None])
    arrived, down, grad_gate = lax.optimization_barrier((arrived, down, grad_gate))
    summed = pl.pallas_call(
        functools.partial(chips_kernel, n_chip, slots),
        in_specs=[VM] * (n_chip + 2),
        out_specs=[VM] * n_e,
        out_shape=[sds((2 * tok, width), BF)] * n_e,
        scratch_shapes=[pltpu.VMEM(block_shape, F32)],
        compiler_params=params(small),
        name="chips",
    )(info, other, parts[0], *arrived)
    home = [summed[0]] + [
        swap(summed[k], 0, k, 1) for k in sorted(range(1, n_e), key=lambda k: (k != n_e // 2, -k))
    ]
    grad_down, grad_up = grads(
        [(0, 18 * part, f), (1, 0, f)], [hidden, gpu], [dys, xs], [down, None]
    )
    home, grad_down, grad_up = lax.optimization_barrier((home, grad_down, grad_up))
    mixed, grad_tokens = pl.pallas_call(
        home_kernel,
        in_specs=[VM] * n_e,
        out_specs=[VM] * 2,
        out_shape=[sds((tok, width), BF)] * 2,
        compiler_params=params(4),
        name="home",
    )(*home)
    return mixed, grad_tokens, grad_gate[None], grad_up[None], grad_down[None]


def solution(mesh):
    return jax.shard_map(
        per_device,
        mesh=mesh,
        in_specs=(
            P("dp", "expert"),
            P("dp", "expert"),
            P("dp", None),
            P("dp", None),
            P("expert", "dp", None),
            P("expert", "dp", None),
            P("expert", "dp", None),
        ),
        out_specs=(
            P("dp", "expert"),
            P("dp", "expert"),
            P("expert", "dp", None),
            P("expert", "dp", None),
            P("expert", "dp", None),
        ),
        check_vma=False,
    )
```
